512 devices in a mesh: box: 32 (over y, x, core), dir: 16 (over z).
Axes of the slice: x: 4, y: 4, z: 16, core: 2. Of those that a mesh axis runs over, the one named last changes fastest.
Arguments:
- current: float32 [2, 1024, 128], P(None, 'box'), may hold values from -6 to 6
- near_block: float32 [2, 1024, 6, 128, 128], P(None, 'box', None, 'dir'), may hold values from -0.15625 to 0.15625
- neighbours: int32 [1024, 6], P('box'), may hold values from 0 to 1023, as said below
- near_count: int32 [1024], P('box'), may hold values from 1 to 6
- radiation: float32 [2, 2, 1024, 128, 512], P(None, None, 'box', 'dir'), may hold values from -0.1875 to 0.1875
- stencil: int32 [2048, 4], P('dir'), may hold values from 0 to 511, as said below
- stencil_weight: float32 [2048, 4], P('dir'), may hold values from -3 to 3
- child_shift: float32 [2, 8, 2048], P(None, None, 'dir'), may hold values from -4 to 4
- list_source: int32 [128, 16], replicated, may hold values from 0 to 127
- list_kind: int32 [128, 16], replicated, may hold values from 0 to 7
- list_count: int32 [128], replicated, may hold values from 1 to 16
- translation: float32 [2, 8, 2048], P(None, None, 'dir'), may hold values from -0.4 to 0.4
Outputs:
- field: float32 [2, 1024, 128], P(None, 'box', 'dir')
The draws below stay inside these ranges and needn't reach their ends.
Inputs may be any that keep to these rules, and one draw needn't show every extreme that they name: `neighbours`: slot 0 of each leaf box is the box itself; every entry lies within 32 leaf boxes of its row's box. `stencil`: entry (q, i) lies between one below and two above q * 512 // 2048, taken modulo 512.
All inputs are finite; a program needn't handle non-finite values.
Results may differ from the reference program's by a relative error of at most 0.0003.
Values sent between devices are 32-bit elements; how exact they have to be, the bound alone decides.
No kernel may reach another device: no remote copies, remote signals or barrier semaphores. Data moves between devices by JAX's collectives and lax.ppermute only.
A program may use at most 64 MiB of HBM per device.

```python
import jax
import jax.numpy as jnp
from jax import lax

BOX_DEV = 32
UNK = 128
NEAR = 6
K0 = 512
K1 = 2048
STENCIL = 4
LIST = 16
KINDS = 8
LEAVES = 1024
TOPS = 128


def draw_neighbours(key, part):
    key = jax.random.fold_in(key, 11)
    leaf_rows = jnp.arange(LEAVES, dtype=jnp.int32)[:, None]
    offsets = jax.random.randint(key, (LEAVES, NEAR), -BOX_DEV, BOX_DEV + 1, dtype=jnp.int32)
    slot_index = jnp.arange(NEAR, dtype=jnp.int32)[None, :]
    offsets = jnp.where(slot_index == 0, 0, offsets)
    target = jnp.clip(leaf_rows + offsets, 0, LEAVES - 1)
    target = target.at[0, 1].set(BOX_DEV)
    target = target.at[LEAVES - 1, 1].set(LEAVES - 1 - BOX_DEV)
    return target.astype(jnp.int32)


def draw_near_count(key, part):
    key = jax.random.fold_in(key, 12)
    counts = jax.random.randint(key, (LEAVES,), 1, NEAR + 1, dtype=jnp.int32)
    counts = counts.at[0].set(NEAR)
    counts = counts.at[1].set(1)
    return counts


def draw_stencil(key, part):
    key = jax.random.fold_in(key, 13)
    centre = jnp.arange(K1, dtype=jnp.int32) * K0 // K1
    offsets = jax.random.randint(key, (K1, STENCIL), -1, 3, dtype=jnp.int32)
    offsets = offsets.at[0, 0].set(-1)
    offsets = offsets.at[0, 1].set(0)
    return ((centre[:, None] + offsets + K0) % K0).astype(jnp.int32)


def draw_list_count(key, part):
    key = jax.random.fold_in(key, 14)
    counts = jax.random.randint(key, (TOPS,), 1, LIST + 1, dtype=jnp.int32)
    counts = counts.at[0].set(LIST)
    counts = counts.at[1].set(1)
    return counts


def with_ends(entries, stream_key, smallest, largest):
    longest = entries.shape.index(max(entries.shape))
    spots = []
    for shift in (0, 1):
        where = [jax.random.randint(jax.random.fold_in(stream_key, axis), (), 0, length) for axis, length in enumerate(entries.shape)]
        where[longest] = (where[longest] + shift) % entries.shape[longest]
        spots.append(tuple(where))
    return entries.at[spots[0]].set(smallest).at[spots[1]].set(largest)


def block_levels(rng, shape, split, low, largest):
    factor_of = 1.0
    for dim, blocks in split:
        steps = jax.random.uniform(jax.random.fold_in(jax.random.fold_in(rng, 6), dim), (blocks,), jnp.float32, low / len(split), largest / len(split))
        factor_of = factor_of * jnp.repeat(jnp.exp(steps), shape[dim] // blocks).reshape((-1,) + (1,) * (len(shape) - 1 - dim))
    return factor_of


def bell_draw(key, dims, deviation, bound, cuts=(), kind=jnp.bfloat16):
    entries = deviation * jax.random.normal(key, dims, jnp.float32)
    if cuts:
        entries = entries * block_levels(key, dims, cuts, -0.22, 0.18)
    return jnp.clip(entries, -bound, bound).astype(kind)


def setup_inputs(seed: int = 0) -> dict:
    streams_of = jax.random.split(jax.random.key(seed), 13)
    current = bell_draw(streams_of[0], (2, LEAVES, UNK), 1.0, 6.0, ((1, 32),), jnp.float32)
    near_block = bell_draw(streams_of[1], (2, LEAVES, NEAR, UNK, UNK), (2 * UNK * NEAR) ** -0.5, 0.15625, ((1, 32), (3, 16)), jnp.float32)
    neighbours = draw_neighbours(jax.random.fold_in(streams_of[12], 71), 0)
    near_count = draw_near_count(jax.random.fold_in(streams_of[12], 71), 0)
    radiation = bell_draw(streams_of[4], (2, 2, LEAVES, UNK, K0), (2 * K0) ** -0.5, 0.1875, ((2, 32), (3, 16)), jnp.float32)
    stencil = draw_stencil(jax.random.fold_in(streams_of[12], 71), 0)
    stencil_weight = bell_draw(streams_of[6], (K1, STENCIL), 0.5, 3.0, ((0, 16),), jnp.float32)
    child_shift = bell_draw(streams_of[7], (2, 8, K1), 0.7, 4.0, ((2, 16),), jnp.float32)
    list_source = with_ends(jax.random.randint(streams_of[8], (TOPS, LIST), 0, TOPS), jax.random.fold_in(streams_of[8], 1), 0, TOPS - 1).astype(jnp.int32)
    list_kind = with_ends(jax.random.randint(streams_of[9], (TOPS, LIST), 0, KINDS), jax.random.fold_in(streams_of[9], 1), 0, KINDS - 1).astype(jnp.int32)
    list_count = draw_list_count(jax.random.fold_in(streams_of[12], 71), 0)
    translation = bell_draw(streams_of[11], (2, KINDS, K1), 0.06, 0.4, ((2, 16),), jnp.float32)
    return dict(current=current, near_block=near_block, neighbours=neighbours, near_count=near_count, radiation=radiation, stencil=stencil, stencil_weight=stencil_weight, child_shift=child_shift, list_source=list_source, list_kind=list_kind, list_count=list_count, translation=translation)


highest = lax.Precision.HIGHEST


def complex_apply(form, left_re, left_im, right_re, right_im):
    real_part = jnp.einsum(form, left_re, right_re, precision=highest) - jnp.einsum(form, left_im, right_im, precision=highest)
    imag_part = jnp.einsum(form, left_re, right_im, precision=highest) + jnp.einsum(form, left_im, right_re, precision=highest)
    return real_part, imag_part


def reference(current, near_block, neighbours, near_count, radiation, stencil, stencil_weight, child_shift, list_source, list_kind, list_count, translation):
    picked = current[:, neighbours, :]
    live = (jnp.arange(NEAR)[None, :] < near_count[:, None]).astype(jnp.float32)
    picked = picked * live[None, :, :, None]
    near_re, near_im = complex_apply("bsuv,bsv->bu", near_block[0], near_block[1], picked[0], picked[1])
    leaf_re, leaf_im = complex_apply("pbuk,bu->pbk", radiation[0], radiation[1], current[0], current[1])
    shift_re, shift_im = child_shift[0], child_shift[1]
    group_re = leaf_re.reshape(2, TOPS, 8, K0).transpose(1, 0, 2, 3)
    group_im = leaf_im.reshape(2, TOPS, 8, K0).transpose(1, 0, 2, 3)

    def lift(pair):
        values_re, values_im = pair
        up_re = jnp.zeros((2, 8, K1), jnp.float32)
        up_im = jnp.zeros((2, 8, K1), jnp.float32)
        for point in range(STENCIL):
            up_re = up_re + jnp.take(values_re, stencil[:, point], axis=2) * stencil_weight[:, point]
            up_im = up_im + jnp.take(values_im, stencil[:, point], axis=2) * stencil_weight[:, point]
        top_re = jnp.sum(up_re * shift_re - up_im * shift_im, axis=1)
        top_im = jnp.sum(up_re * shift_im + up_im * shift_re, axis=1)
        return top_re, top_im

    top_re, top_im = lax.map(lift, (group_re, group_im))

    def couple(args):
        sources, kinds, count = args
        keep = (jnp.arange(LIST) < count).astype(jnp.float32)[:, None]
        source_re = top_re[sources]
        source_im = top_im[sources]
        factor_re = (translation[0][kinds] * keep)[:, None, :]
        factor_im = (translation[1][kinds] * keep)[:, None, :]
        moved_re = jnp.sum(source_re * factor_re - source_im * factor_im, axis=0)
        moved_im = jnp.sum(source_re * factor_im + source_im * factor_re, axis=0)
        return moved_re, moved_im

    moved_re, moved_im = lax.map(couple, (list_source, list_kind, list_count))

    def lower(pair):
        values_re, values_im = pair
        down_re = values_re[:, None, :] * shift_re + values_im[:, None, :] * shift_im
        down_im = values_im[:, None, :] * shift_re - values_re[:, None, :] * shift_im
        total_re = jnp.zeros((2, 8, K0), jnp.float32)
        total_im = jnp.zeros((2, 8, K0), jnp.float32)
        for point in range(STENCIL):
            total_re = total_re.at[:, :, stencil[:, point]].add(down_re * stencil_weight[:, point])
            total_im = total_im.at[:, :, stencil[:, point]].add(down_im * stencil_weight[:, point])
        return total_re, total_im

    income_re, income_im = lax.map(lower, (moved_re, moved_im))
    income_re = income_re.transpose(1, 0, 2, 3).reshape(2, LEAVES, K0)
    income_im = income_im.transpose(1, 0, 2, 3).reshape(2, LEAVES, K0)
    far_re = jnp.einsum("pbuk,pbk->bu", radiation[0], income_re, precision=highest) + jnp.einsum("pbuk,pbk->bu", radiation[1], income_im, precision=highest)
    far_im = jnp.einsum("pbuk,pbk->bu", radiation[0], income_im, precision=highest) - jnp.einsum("pbuk,pbk->bu", radiation[1], income_re, precision=highest)
    return jnp.stack([near_re + far_re, near_im + far_im])
```

```python
import functools

import jax
import jax.numpy as jnp
from jax import lax
from jax.experimental import pallas as pl
from jax.experimental.pallas import tpu as pltpu
from jax.sharding import PartitionSpec as P

highest = lax.Precision.HIGHEST
f32 = jnp.float32
below, above = 1, 2
lead = 8
VMEM = pl.BlockSpec(memory_space=pltpu.VMEM)
SMEM = pl.BlockSpec(memory_space=pltpu.SMEM)
ANY = pl.BlockSpec(memory_space=pl.ANY)
params = pltpu.CompilerParams(vmem_limit_bytes=12 * 2**20)


def leaf_kernel(cuts, shares, current, stencil, weight, radiation, out, interp, patterns, columns, rows, samples, sems):
    pols, boxes, own, width = radiation.shape[1:]
    place = lax.axis_index("dir")
    step = boxes // cuts
    copies = []
    for cut in range(cuts):
        part = pl.ds(cut * step, step)
        copy = pltpu.make_async_copy(radiation.at[:, :, part], patterns.at[:, :, part], sems.at[cut])
        copy.start()
        copies.append(copy)
    piece = width // shares
    lanes = stencil.shape[1]
    row = lax.broadcasted_iota(jnp.int32, (128, lanes), 0)
    table = jnp.zeros((128, lanes), f32)
    for point in range(stencil.shape[0]):
        at = lax.rem(stencil[point : point + 1, :] - (place * piece - below) + width, width)
        table = table + jnp.where(row == at, weight[point : point + 1, :], 0.0)
    interp[...] = table
    for part in range(2):
        columns[part] = current[part].T
    mine = pl.ds(pl.multiple_of(place * own, own), own)
    real, imag = columns[0, mine, :], columns[1, mine, :]
    for cut in range(cuts):
        copies[cut].wait()
        for box in range(cut * step, (cut + 1) * step):
            cur_re, cur_im = real[:, box : box + 1], imag[:, box : box + 1]
            for pol in range(pols):
                rad_re, rad_im = patterns[0, pol, box], patterns[1, pol, box]
                at = pol * boxes + box
                rows[at : at + 1, :] = jnp.sum(rad_re * cur_re - rad_im * cur_im, axis=0, keepdims=True)
                at = (pols + pol) * boxes + box
                rows[at : at + 1, :] = jnp.sum(rad_re * cur_im + rad_im * cur_re, axis=0, keepdims=True)
    for block in range(width // 128):
        samples[lead + block * 128 : lead + block * 128 + 128, :] = rows[:, block * 128 : block * 128 + 128].T
    samples[lead - below : lead, :] = samples[lead + width - below : lead + width, :]
    samples[lead + width : lead + width + above, :] = samples[lead : lead + above, :]
    span = piece + below + above
    for share in range(shares):
        first = lead - below + share * piece
        out[share * span : (share + 1) * span, :] = samples[first : first + span, :]


def lift_kernel(shares, copies, received, interp, shift, out, total, tops):
    span = received.shape[0] // shares
    total[...] = jnp.zeros_like(total)
    part = received[0:span, :]
    for share in range(1, shares):
        part = part + received[share * span : (share + 1) * span, :]
    total[0:span, :] = part
    up = jnp.dot(total[...].T, interp[...], precision=highest, preferred_element_type=f32)
    shift_re, shift_im = shift[0], shift[1]
    half = up.shape[0] // 2
    lines = half // 8
    for line in range(lines):
        up_re, up_im = up[line * 8 : line * 8 + 8], up[half + line * 8 : half + line * 8 + 8]
        tops[line : line + 1, :] = jnp.sum(up_re * shift_re - up_im * shift_im, axis=0, keepdims=True)
        tops[lines + line : lines + line + 1, :] = jnp.sum(up_re * shift_im + up_im * shift_re, axis=0, keepdims=True)
    value = tops[...]
    for copy in range(copies):
        out[copy * 2 * lines : (copy + 1) * 2 * lines, :] = value


def lower_kernel(shares, span, parents, source, kind, count, received, translation, interp, shift, out, factors, down):
    kinds = translation.shape[1]
    lines = down.shape[0] // 16
    pols = lines // parents
    first = lax.axis_index("box") * parents
    factors[...] = jnp.zeros_like(factors)
    factors[:, 0:kinds, :] = translation[...]
    shift_re, shift_im = shift[0], shift[1]
    for parent in range(parents):
        used = count[first + parent]
        by_re = jnp.zeros((2 * pols, 128), f32)
        by_im = jnp.zeros((2 * pols, 128), f32)
        for slot in range(source.shape[0]):
            origin = source[slot, first + parent]
            which = jnp.where(slot < used, kind[slot, first + parent], kinds)
            begin = (origin // parents) * (2 * lines) + lax.rem(origin, parents)
            tops = received[pl.ds(begin, 2 * pols, stride=parents), :]
            by_re = by_re + tops * factors[0, pl.ds(which, 1), :]
            by_im = by_im + tops * factors[1, pl.ds(which, 1), :]
        moved_re = by_re[0:pols] - by_im[pols:]
        moved_im = by_im[0:pols] + by_re[pols:]
        for pol in range(pols):
            mine_re, mine_im = moved_re[pol : pol + 1], moved_im[pol : pol + 1]
            at = (pol * parents + parent) * 8
            down[at : at + 8, :] = mine_re * shift_re + mine_im * shift_im
            down[lines * 8 + at : lines * 8 + at + 8, :] = mine_im * shift_re - mine_re * shift_im
    settled = lax.dot_general(
        interp[0:40, :], down[...], (((1,), (1,)), ((), ())), precision=highest, preferred_element_type=f32
    )
    value = settled[0:span]
    for share in range(shares):
        out[share * span : (share + 1) * span, :] = value


def near_kernel(neighbours, near_count, low, current, high, blocks, out, padded):
    slots, boxes = neighbours.shape
    first = lax.axis_index("box") * boxes - boxes
    for part in range(2):
        padded[part, 0:boxes, :] = low[part]
        padded[part, boxes : 2 * boxes, :] = current[part]
        padded[part, 2 * boxes : 3 * boxes, :] = high[part]
        padded[part, 3 * boxes :, :] = jnp.zeros((8, 128), f32)
    for box in range(boxes):
        used = near_count[box]
        sum_re = jnp.zeros(out.shape[2:], f32)
        sum_im = jnp.zeros(out.shape[2:], f32)
        for slot in range(slots):
            at = jnp.where(slot < used, neighbours[slot, box] - first, 3 * boxes)
            cur_re, cur_im = padded[0, pl.ds(at, 1), :], padded[1, pl.ds(at, 1), :]
            block_re, block_im = blocks[0, box, slot], blocks[1, box, slot]
            sum_re = sum_re + (block_re * cur_re - block_im * cur_im)
            sum_im = sum_im + (block_re * cur_im + block_im * cur_re)
        out[0, box] = sum_re
        out[1, box] = sum_im


def field_kernel(shares, received, radiation, near, out, samples, rows):
    pols, boxes, own, width = radiation.shape[1:]
    span = received.shape[0] // shares
    piece = width // shares
    samples[...] = jnp.zeros_like(samples)
    for share in range(shares):
        first = lead - below + share * piece
        samples[first : first + span, :] += received[share * span : (share + 1) * span, :]
    samples[lead + width - below : lead + width, :] += samples[lead - below : lead, :]
    samples[lead : lead + above, :] += samples[lead + width : lead + width + above, :]
    for block in range(width // 128):
        rows[:, block * 128 : block * 128 + 128] = samples[lead + block * 128 : lead + block * 128 + 128, :].T
    lane = lax.broadcasted_iota(jnp.int32, (own, boxes), 1)
    all_re = jnp.zeros((own, boxes), f32)
    all_im = jnp.zeros((own, boxes), f32)
    for box in range(boxes):
        sum_re, sum_im = near[0, box], near[1, box]
        for pol in range(pols):
            at_re, at_im = pol * boxes + box, (pols + pol) * boxes + box
            for block in range(width // 128):
                cut = slice(block * 128, block * 128 + 128)
                in_re, in_im = rows[at_re : at_re + 1, cut], rows[at_im : at_im + 1, cut]
                rad_re, rad_im = radiation[0, pol, box, :, cut], radiation[1, pol, box, :, cut]
                sum_re = sum_re + (rad_re * in_re + rad_im * in_im)
                sum_im = sum_im + (rad_re * in_im - rad_im * in_re)
        all_re = jnp.where(lane == box, jnp.sum(sum_re, axis=1, keepdims=True), all_re)
        all_im = jnp.where(lane == box, jnp.sum(sum_im, axis=1, keepdims=True), all_im)
    out[0] = all_re
    out[1] = all_im


def local(
    current,
    near_block,
    neighbours,
    near_count,
    radiation,
    stencil,
    stencil_weight,
    child_shift,
    list_source,
    list_kind,
    list_count,
    translation,
):
    box_total, dir_total = lax.axis_size("box"), lax.axis_size("dir")
    _, pols, boxes, own, width = radiation.shape
    share = stencil.shape[0]
    parents = boxes // 8
    piece = width // dir_total
    span = piece + below + above
    lanes = 2 * pols * boxes
    held = lead + width + 8
    cuts = 4
    shape = functools.partial(jax.ShapeDtypeStruct, dtype=f32)

    forward = [(i, i + 1) for i in range(box_total - 1)]
    low = lax.ppermute(current, "box", forward)
    high = lax.ppermute(current, "box", [(b, a) for a, b in forward])

    windows, interp = pl.pallas_call(
        functools.partial(leaf_kernel, cuts, dir_total),
        out_shape=(shape((dir_total * span, lanes)), shape((128, share))),
        in_specs=[VMEM, VMEM, VMEM, ANY],
        out_specs=(VMEM, VMEM),
        scratch_shapes=[
            pltpu.VMEM(radiation.shape, f32),
            pltpu.VMEM((2, current.shape[2], boxes), f32),
            pltpu.VMEM((lanes, width), f32),
            pltpu.VMEM((held, lanes), f32),
            pltpu.SemaphoreType.DMA((cuts,)),
        ],
        compiler_params=params,
        name="leaf",
    )(current, stencil.T, stencil_weight.T, radiation)
    windows = lax.all_to_all(windows.reshape(dir_total, 1, span * lanes), "dir", 0, 0, tiled=True)

    tops = pl.pallas_call(
        functools.partial(lift_kernel, dir_total, box_total),
        out_shape=shape((box_total * lanes // 8, share)),
        in_specs=[VMEM] * 3,
        out_specs=VMEM,
        scratch_shapes=[pltpu.VMEM((128, lanes), f32), pltpu.VMEM((lanes // 8, share), f32)],
        compiler_params=params,
        name="lift",
    )(windows.reshape(dir_total * span, lanes), interp, child_shift)
    tops = lax.all_to_all(tops.reshape(box_total, 1, lanes // 8 * share), "box", 0, 0, tiled=True)

    near = pl.pallas_call(
        near_kernel,
        out_shape=shape((2, boxes, own, 128)),
        in_specs=[SMEM, SMEM] + [VMEM] * 4,
        out_specs=VMEM,
        scratch_shapes=[pltpu.VMEM((2, 3 * boxes + 8, 128), f32)],
        compiler_params=params,
        name="near",
    )(neighbours.T, near_count, low, current, high, near_block)

    income = pl.pallas_call(
        functools.partial(lower_kernel, dir_total, span, parents),
        out_shape=shape((dir_total * span, lanes)),
        in_specs=[SMEM] * 3 + [VMEM] * 4,
        out_specs=VMEM,
        scratch_shapes=[pltpu.VMEM((2, 16, share), f32), pltpu.VMEM((lanes, share), f32)],
        compiler_params=params,
        name="lower",
    )(list_source.T, list_kind.T, list_count, tops.reshape(-1, share), translation, interp, child_shift)
    income = lax.all_to_all(income.reshape(dir_total, 1, span * lanes), "dir", 0, 0, tiled=True)

    field = pl.pallas_call(
        functools.partial(field_kernel, dir_total),
        out_shape=shape((2, own, boxes)),
        in_specs=[VMEM] * 3,
        out_specs=VMEM,
        scratch_shapes=[pltpu.VMEM((held, lanes), f32), pltpu.VMEM((lanes, width), f32)],
        compiler_params=params,
        name="field",
    )(income.reshape(dir_total * span, lanes), radiation, near)
    return field.transpose(0, 2, 1)


def solution(mesh):
    return jax.shard_map(
        local,
        mesh=mesh,
        in_specs=(
            P(None, "box", None),
            P(None, "box", None, "dir", None),
            P("box", None),
            P("box"),
            P(None, None, "box", "dir", None),
            P("dir", None),
            P("dir", None),
            P(None, None, "dir"),
            P(),
            P(),
            P(),
            P(None, None, "dir"),
        ),
        out_specs=P(None, "box", "dir"),
        check_vma=False,
    )
```

```python
import functools

import jax
import jax.numpy as jnp
from jax import lax
from jax.experimental import pallas as pl
from jax.experimental.pallas import tpu as pltpu
from jax.sharding import PartitionSpec as P

highest = lax.Precision.HIGHEST
f32 = jnp.float32
below, above = 1, 2
lead = 8
VMEM = pl.BlockSpec(memory_space=pltpu.VMEM)
SMEM = pl.BlockSpec(memory_space=pltpu.SMEM)
ANY = pl.BlockSpec(memory_space=pl.ANY)
HBM = pl.BlockSpec(memory_space=pltpu.HBM)
params = pltpu.CompilerParams(vmem_limit_bytes=12 * 2**20)
alone = pltpu.CompilerParams(vmem_limit_bytes=60 * 2**20)


def leaf_kernel(cuts, shares, current, radiation, out, patterns, given, columns, rows, samples, sems):
    pols, boxes, own, width = radiation.shape[1:]
    step = boxes // cuts
    first = pltpu.make_async_copy(current, given, sems.at[cuts])
    first.start()
    copies = []
    for cut in range(cuts):
        part = pl.ds(cut * step, step)
        copy = pltpu.make_async_copy(radiation.at[:, :, part], patterns.at[:, :, part], sems.at[cut])
        copy.start()
        copies.append(copy)
    first.wait()
    for part in range(2):
        columns[part] = given[part].T
    mine = pl.ds(pl.multiple_of(lax.axis_index("dir") * own, own), own)
    real, imag = columns[0, mine, :], columns[1, mine, :]
    for cut in range(cuts):
        copies[cut].wait()
        for box in range(cut * step, (cut + 1) * step):
            cur_re, cur_im = real[:, box : box + 1], imag[:, box : box + 1]
            for pol in range(pols):
                rad_re, rad_im = patterns[0, pol, box], patterns[1, pol, box]
                at = pol * boxes + box
                rows[at : at + 1, :] = jnp.sum(rad_re * cur_re - rad_im * cur_im, axis=0, keepdims=True)
                at = (pols + pol) * boxes + box
                rows[at : at + 1, :] = jnp.sum(rad_re * cur_im + rad_im * cur_re, axis=0, keepdims=True)
    for block in range(width // 128):
        samples[lead + block * 128 : lead + block * 128 + 128, :] = rows[:, block * 128 : block * 128 + 128].T
    samples[lead - below : lead, :] = samples[lead + width - below : lead + width, :]
    samples[lead + width : lead + width + above, :] = samples[lead : lead + above, :]
    piece = width // shares
    span = piece + below + above
    for share in range(shares):
        begin = lead - below + share * piece
        out[share * span : (share + 1) * span, :] = samples[begin : begin + span, :]


def plan_kernel(parents, width, piece, stencil, weight, source, kind, count, translation, interp, picks, factors, codes):
    lanes = stencil.shape[1]
    begin = lax.axis_index("dir") * piece - below
    row = lax.broadcasted_iota(jnp.int32, (128, lanes), 0)
    table = jnp.zeros((128, lanes), f32)
    for point in range(stencil.shape[0]):
        at = lax.rem(stencil[point : point + 1, :] - begin + width, width)
        table = table + jnp.where(row == at, weight[point : point + 1, :], 0.0)
    interp[...] = table
    kinds = translation.shape[1]
    slots, tops = source.shape
    lines, columns = picks.shape[0] // (kinds * parents), picks.shape[1]
    origin = source[...]
    spot = (origin // parents) * (lines * parents) + lax.rem(origin, parents)
    live = lax.broadcasted_iota(jnp.int32, (slots, tops), 0) < count[...]
    codes[...] = jnp.where(live, kind[...] * columns + spot, -1).astype(f32).T
    mine = codes[pl.ds(lax.axis_index("box") * parents, parents), :]
    own_kind = lax.broadcasted_iota(jnp.int32, (kinds * parents, slots), 0) // parents
    mine = jnp.concatenate([mine] * kinds, axis=0) - (own_kind * columns).astype(f32)
    lane = lax.broadcasted_iota(jnp.int32, (kinds * parents, columns), 1).astype(f32)
    counts = jnp.zeros((kinds * parents, columns), f32)
    for slot in range(slots):
        counts = counts + jnp.where(mine[:, slot : slot + 1] == lane, 1.0, 0.0)
    parts = [pltpu.roll(counts, line * parents, 1) if line else counts for line in range(lines)]
    picks[...] = jnp.concatenate(parts, axis=0).astype(jnp.bfloat16)
    for part in range(2):
        for which in range(kinds):
            one = translation[part, which : which + 1, :]
            factors[part, which * parents : (which + 1) * parents, :] = jnp.broadcast_to(one, (parents, lanes))


def lift_kernel(shares, copies, received, interp, shift, near, out, total, tops):
    span = received.shape[0] // shares
    total[...] = jnp.zeros_like(total)
    part = received[0:span, :]
    for share in range(1, shares):
        part = part + received[share * span : (share + 1) * span, :]
    total[0:span, :] = part
    up = jnp.dot(total[...].T, interp[...], precision=highest, preferred_element_type=f32)
    shift_re, shift_im = shift[0], shift[1]
    half = up.shape[0] // 2
    lines = half // 8
    for line in range(lines):
        up_re, up_im = up[line * 8 : line * 8 + 8], up[half + line * 8 : half + line * 8 + 8]
        tops[line : line + 1, :] = jnp.sum(up_re * shift_re - up_im * shift_im, axis=0, keepdims=True)
        tops[lines + line : lines + line + 1, :] = jnp.sum(up_re * shift_im + up_im * shift_re, axis=0, keepdims=True)
    value = tops[...]
    for copy in range(copies):
        out[copy * 2 * lines : (copy + 1) * 2 * lines, :] = value


def lower_kernel(shares, span, parents, picks, factors, received, interp, shift, out, down):
    lines = down.shape[0] // 16
    pols = lines // parents
    each = factors.shape[1]
    rest = received[...]
    table = picks[...]
    raw = jnp.zeros((table.shape[0], rest.shape[1]), f32)
    for _ in range(3):
        part = rest.astype(jnp.bfloat16)
        raw = raw + jnp.dot(table, part, preferred_element_type=f32)
        rest = rest - part.astype(f32)

    def over_kinds(line, part):
        terms = raw[line * each : (line + 1) * each] * factors[part]
        total = terms[0:parents]
        for which in range(1, each // parents):
            total = total + terms[which * parents : (which + 1) * parents]
        return total

    shift_re, shift_im = shift[0], shift[1]
    for pol in range(pols):
        moved_re = over_kinds(pol, 0) - over_kinds(pols + pol, 1)
        moved_im = over_kinds(pol, 1) + over_kinds(pols + pol, 0)
        for parent in range(parents):
            mine_re, mine_im = moved_re[parent : parent + 1], moved_im[parent : parent + 1]
            at = (pol * parents + parent) * 8
            down[at : at + 8, :] = mine_re * shift_re + mine_im * shift_im
            down[lines * 8 + at : lines * 8 + at + 8, :] = mine_im * shift_re - mine_re * shift_im
    settled = lax.dot_general(
        interp[0:40, :], down[...], (((1,), (1,)), ((), ())), precision=highest, preferred_element_type=f32
    )
    value = settled[0:span]
    for share in range(shares):
        out[share * span : (share + 1) * span, :] = value


def near_kernel(neighbours, near_count, low, current, high, blocks, out, padded):
    slots, boxes = neighbours.shape
    first = lax.axis_index("box") * boxes - boxes
    for part in range(2):
        padded[part, 0:boxes, :] = low[part]
        padded[part, boxes : 2 * boxes, :] = current[part]
        padded[part, 2 * boxes : 3 * boxes, :] = high[part]
        padded[part, 3 * boxes :, :] = jnp.zeros((8, 128), f32)
    for box in range(boxes):
        used = near_count[box]
        sum_re = jnp.zeros(out.shape[2:], f32)
        sum_im = jnp.zeros(out.shape[2:], f32)
        for slot in range(slots):
            at = jnp.where(slot < used, neighbours[slot, box] - first, 3 * boxes)
            cur_re, cur_im = padded[0, pl.ds(at, 1), :], padded[1, pl.ds(at, 1), :]
            block_re, block_im = blocks[0, box, slot], blocks[1, box, slot]
            sum_re = sum_re + (block_re * cur_re - block_im * cur_im)
            sum_im = sum_im + (block_re * cur_im + block_im * cur_re)
        out[0, box] = sum_re
        out[1, box] = sum_im


def field_kernel(shares, received, radiation, near, out, samples, rows):
    pols, boxes, own, width = radiation.shape[1:]
    span = received.shape[0] // shares
    piece = width // shares
    samples[...] = jnp.zeros_like(samples)
    for share in range(shares):
        first = lead - below + share * piece
        samples[first : first + span, :] += received[share * span : (share + 1) * span, :]
    samples[lead + width - below : lead + width, :] += samples[lead - below : lead, :]
    samples[lead : lead + above, :] += samples[lead + width : lead + width + above, :]
    for block in range(width // 128):
        rows[:, block * 128 : block * 128 + 128] = samples[lead + block * 128 : lead + block * 128 + 128, :].T
    lane = lax.broadcasted_iota(jnp.int32, (own, boxes), 1)
    all_re = jnp.zeros((own, boxes), f32)
    all_im = jnp.zeros((own, boxes), f32)
    for box in range(boxes):
        sum_re, sum_im = near[0, box], near[1, box]
        for pol in range(pols):
            at_re, at_im = pol * boxes + box, (pols + pol) * boxes + box
            for block in range(width // 128):
                cut = slice(block * 128, block * 128 + 128)
                in_re, in_im = rows[at_re : at_re + 1, cut], rows[at_im : at_im + 1, cut]
                rad_re, rad_im = radiation[0, pol, box, :, cut], radiation[1, pol, box, :, cut]
                sum_re = sum_re + (rad_re * in_re + rad_im * in_im)
                sum_im = sum_im + (rad_re * in_im - rad_im * in_re)
        all_re = jnp.where(lane == box, jnp.sum(sum_re, axis=1, keepdims=True), all_re)
        all_im = jnp.where(lane == box, jnp.sum(sum_im, axis=1, keepdims=True), all_im)
    out[0] = all_re
    out[1] = all_im


def local(
    current,
    near_block,
    neighbours,
    near_count,
    radiation,
    stencil,
    stencil_weight,
    child_shift,
    list_source,
    list_kind,
    list_count,
    translation,
):
    box_total, dir_total = lax.axis_size("box"), lax.axis_size("dir")
    _, pols, boxes, own, width = radiation.shape
    share = stencil.shape[0]
    parents = boxes // 8
    piece = width // dir_total
    span = piece + below + above
    lanes = 2 * pols * boxes
    held = lead + width + 8
    cuts = 4

    def shape(dims, dtype=f32):
        return jax.ShapeDtypeStruct(dims, dtype)

    forward = [(i, i + 1) for i in range(box_total - 1)]
    low = lax.ppermute(current, "box", forward)
    high = lax.ppermute(current, "box", [(b, a) for a, b in forward])

    windows = pl.pallas_call(
        functools.partial(leaf_kernel, cuts, dir_total),
        out_shape=shape((dir_total * span, lanes)),
        in_specs=[HBM, HBM],
        out_specs=VMEM,
        scratch_shapes=[
            pltpu.VMEM(radiation.shape, f32),
            pltpu.VMEM(current.shape, f32),
            pltpu.VMEM((2, current.shape[2], boxes), f32),
            pltpu.VMEM((lanes, width), f32),
            pltpu.VMEM((held, lanes), f32),
            pltpu.SemaphoreType.DMA((cuts + 1,)),
        ],
        compiler_params=alone,
        name="leaf",
    )(current, radiation)
    windows = lax.all_to_all(windows.reshape(dir_total, 1, span * lanes), "dir", 0, 0, tiled=True)

    kinds, tops_total = translation.shape[1], list_source.shape[0]
    interp, picks, factors = pl.pallas_call(
        functools.partial(plan_kernel, parents, width, piece),
        out_shape=(
            shape((128, share)),
            shape((2 * pols * kinds * parents, box_total * lanes // 8), dtype=jnp.bfloat16),
            shape((2, kinds * parents, share)),
        ),
        in_specs=[VMEM] * 6,
        out_specs=(VMEM, VMEM, VMEM),
        scratch_shapes=[pltpu.VMEM((tops_total, list_source.shape[1]), f32)],
        compiler_params=params,
        cost_estimate=pl.CostEstimate(flops=2_000_000, bytes_accessed=2_000_000, transcendentals=0),
        name="plan",
    )(stencil.T, stencil_weight.T, list_source.T, list_kind.T, list_count.reshape(1, -1), translation)

    near = pl.pallas_call(
        near_kernel,
        out_shape=shape((2, boxes, own, 128)),
        in_specs=[SMEM, SMEM] + [VMEM] * 4,
        out_specs=VMEM,
        scratch_shapes=[pltpu.VMEM((2, 3 * boxes + 8, 128), f32)],
        compiler_params=params,
        cost_estimate=pl.CostEstimate(flops=4_000_000, bytes_accessed=4_000_000, transcendentals=0),
        name="near",
    )(neighbours.T, near_count, low, current, high, near_block)

    tops = pl.pallas_call(
        functools.partial(lift_kernel, dir_total, box_total),
        out_shape=shape((box_total * lanes // 8, share)),
        in_specs=[VMEM] * 3 + [ANY],
        out_specs=VMEM,
        scratch_shapes=[pltpu.VMEM((128, lanes), f32), pltpu.VMEM((lanes // 8, share), f32)],
        compiler_params=params,
        name="lift",
    )(windows.reshape(dir_total * span, lanes), interp, child_shift, near)
    tops = lax.all_to_all(tops.reshape(box_total, 1, lanes // 8 * share), "box", 0, 0, tiled=True)

    income = pl.pallas_call(
        functools.partial(lower_kernel, dir_total, span, parents),
        out_shape=shape((dir_total * span, lanes)),
        in_specs=[VMEM] * 5,
        out_specs=VMEM,
        scratch_shapes=[pltpu.VMEM((lanes, share), f32)],
        compiler_params=params,
        name="lower",
    )(picks, factors, tops.reshape(-1, share), interp, child_shift)
    income = lax.all_to_all(income.reshape(dir_total, 1, span * lanes), "dir", 0, 0, tiled=True)

    field = pl.pallas_call(
        functools.partial(field_kernel, dir_total),
        out_shape=shape((2, own, boxes)),
        in_specs=[VMEM] * 3,
        out_specs=VMEM,
        scratch_shapes=[pltpu.VMEM((held, lanes), f32), pltpu.VMEM((lanes, width), f32)],
        compiler_params=params,
        name="field",
    )(income.reshape(dir_total * span, lanes), radiation, near)
    return field.transpose(0, 2, 1)


def solution(mesh):
    return jax.shard_map(
        local,
        mesh=mesh,
        in_specs=(
            P(None, "box", None),
            P(None, "box", None, "dir", None),
            P("box", None),
            P("box"),
            P(None, None, "box", "dir", None),
            P("dir", None),
            P("dir", None),
            P(None, None, "dir"),
            P(),
            P(),
            P(),
            P(None, None, "dir"),
        ),
        out_specs=P(None, "box", "dir"),
        check_vma=False,
    )
```

```python
import functools

import jax
import jax.numpy as jnp
from jax import lax
from jax.experimental import pallas as pl
from jax.experimental.pallas import tpu as pltpu
from jax.sharding import PartitionSpec as P

highest = lax.Precision.HIGHEST
f32 = jnp.float32
below, above = 1, 2
lead = 8
reach = below + above + 1
VMEM = pl.BlockSpec(memory_space=pltpu.VMEM)
SMEM = pl.BlockSpec(memory_space=pltpu.SMEM)
ANY = pl.BlockSpec(memory_space=pl.ANY)
HBM = pl.BlockSpec(memory_space=pltpu.HBM)
params = pltpu.CompilerParams(vmem_limit_bytes=12 * 2**20)
alone = pltpu.CompilerParams(vmem_limit_bytes=60 * 2**20)


def leaf_kernel(cuts, shares, total, spare, current, stencil, weight, shift, radiation, out, patterns, *scratch):
    given, points, weights, shifts, tables, columns, rows, samples, sems = scratch
    pols, boxes, own, width = radiation.shape[1:]
    step = boxes // cuts
    small = [
        pltpu.make_async_copy(source, target, sems.at[cuts + index])
        for index, (source, target) in enumerate(((current, given), (stencil, points), (weight, weights), (shift, shifts)))
    ]
    for copy in small:
        copy.start()
    copies = []
    for cut in range(cuts):
        part = pl.ds(cut * step, step)
        copy = pltpu.make_async_copy(radiation.at[:, :, part], patterns.at[:, :, part], sems.at[cut])
        copy.start()
        copies.append(copy)
    for copy in small:
        copy.wait()
    for part in range(2):
        columns[part] = given[part].T
    place = lax.axis_index("dir")
    mine = pl.ds(pl.multiple_of(place * own, own), own)
    piece = width // shares
    lanes = stencil.shape[1]
    tables[0:8, :] = shifts[0]
    tables[8:16, :] = shifts[1]
    tables[16:, :] = jnp.zeros((tables.shape[0] - 16, lanes), f32)
    centre = place * piece - below + lax.broadcasted_iota(jnp.int32, (1, lanes), 1) // (lanes // piece)
    for offset in range(reach):
        line = jnp.zeros((1, lanes), f32)
        for point in range(stencil.shape[0]):
            at = lax.rem(points[point : point + 1, :] - centre + width, width)
            line = line + jnp.where(at == offset, weights[point : point + 1, :], 0.0)
        tables[16 + offset : 17 + offset, :] = line
    begin = lax.rem(lax.axis_index("box") + total - lax.rem(place * (16 + reach), total), total)
    real, imag = columns[0, mine, :], columns[1, mine, :]
    for cut in range(cuts):
        copies[cut].wait()
        for box in range(cut * step, (cut + 1) * step):
            cur_re, cur_im = real[:, box : box + 1], imag[:, box : box + 1]
            for pol in range(pols):
                rad_re, rad_im = patterns[0, pol, box], patterns[1, pol, box]
                at = pol * boxes + box
                rows[at : at + 1, :] = jnp.sum(rad_re * cur_re - rad_im * cur_im, axis=0, keepdims=True)
                at = (pols + pol) * boxes + box
                rows[at : at + 1, :] = jnp.sum(rad_re * cur_im + rad_im * cur_re, axis=0, keepdims=True)
    for block in range(width // 128):
        samples[lead + block * 128 : lead + block * 128 + 128, :] = rows[:, block * 128 : block * 128 + 128].T
    samples[lead - below : lead, :] = samples[lead + width - below : lead + width, :]
    samples[lead + width : lead + width + above, :] = samples[lead : lead + above, :]
    span = piece + below + above
    own_rows = [tables[pl.ds(begin + index * total, 1), :] for index in range(spare)]
    for share in range(shares):
        first, at = lead - below + share * piece, share * (span + spare)
        out[at : at + span, :] = samples[first : first + span, :]
        for index in range(spare):
            out[at + span + index : at + span + index + 1, :] = own_rows[index]


def plan_kernel(parents, width, piece, stencil, weight, source, kind, count, translation, interp, picks, factors, codes):
    lanes = stencil.shape[1]
    begin = lax.axis_index("dir") * piece - below
    row = lax.broadcasted_iota(jnp.int32, (128, lanes), 0)
    table = jnp.zeros((128, lanes), f32)
    for point in range(stencil.shape[0]):
        at = lax.rem(stencil[point : point + 1, :] - begin + width, width)
        table = table + jnp.where(row == at, weight[point : point + 1, :], 0.0)
    interp[...] = table
    kinds = translation.shape[1]
    slots, tops = source.shape
    lines, columns = picks.shape[0] // (kinds * parents), picks.shape[1]
    origin = source[...]
    spot = (origin // parents) * (lines * parents) + lax.rem(origin, parents)
    live = lax.broadcasted_iota(jnp.int32, (slots, tops), 0) < count[...]
    codes[...] = jnp.where(live, kind[...] * columns + spot, -1).astype(f32).T
    mine = codes[pl.ds(lax.axis_index("box") * parents, parents), :]
    own_kind = lax.broadcasted_iota(jnp.int32, (kinds * parents, slots), 0) // parents
    mine = jnp.concatenate([mine] * kinds, axis=0) - (own_kind * columns).astype(f32)
    lane = lax.broadcasted_iota(jnp.int32, (kinds * parents, columns), 1).astype(f32)
    counts = jnp.zeros((kinds * parents, columns), f32)
    for slot in range(slots):
        counts = counts + jnp.where(mine[:, slot : slot + 1] == lane, 1.0, 0.0)
    parts = [pltpu.roll(counts, line * parents, 1) if line else counts for line in range(lines)]
    picks[...] = jnp.concatenate(parts, axis=0).astype(jnp.bfloat16)
    for part in range(2):
        for which in range(kinds):
            one = translation[part, which : which + 1, :]
            factors[part, which * parents : (which + 1) * parents, :] = jnp.broadcast_to(one, (parents, lanes))


def lift_kernel(shares, copies, spare, received, interp, shift, near, out, total, tops):
    each = received.shape[0] // shares
    span = each - spare
    total[...] = jnp.zeros_like(total)
    part = received[0:span, :]
    for share in range(1, shares):
        part = part + received[share * each : share * each + span, :]
    total[0:span, :] = part
    up = jnp.dot(total[...].T, interp[...], precision=highest, preferred_element_type=f32)
    shift_re, shift_im = shift[0], shift[1]
    half = up.shape[0] // 2
    lines = half // 8
    for line in range(lines):
        up_re, up_im = up[line * 8 : line * 8 + 8], up[half + line * 8 : half + line * 8 + 8]
        tops[line : line + 1, :] = jnp.sum(up_re * shift_re - up_im * shift_im, axis=0, keepdims=True)
        tops[lines + line : lines + line + 1, :] = jnp.sum(up_re * shift_im + up_im * shift_re, axis=0, keepdims=True)
    height = tops.shape[0]
    place = lax.axis_index("box")
    for index in range(height - 2 * lines):
        number = place + index * copies
        share = number // (16 + reach)
        at = share * each + span + (number - share * (16 + reach)) // copies
        tops[2 * lines + index : 2 * lines + index + 1, :] = received[pl.ds(at, 1), :]
    value = tops[...]
    for copy in range(copies):
        out[copy * height : (copy + 1) * height, :] = value


def lower_kernel(shares, parents, picks, factors, gathered, out, compact):
    each = factors.shape[1]
    lines = picks.shape[0] // each
    pols = lines // 2
    height = lines * parents
    boxes = compact.shape[0] // height
    stride = gathered.shape[0] // boxes
    for box in range(boxes):
        compact[box * height : (box + 1) * height, :] = gathered[box * stride : box * stride + height, :]
    rest = compact[...]
    table = picks[...]
    raw = jnp.zeros((table.shape[0], rest.shape[1]), f32)
    for _ in range(3):
        part = rest.astype(jnp.bfloat16)
        raw = raw + jnp.dot(table, part, preferred_element_type=f32)
        rest = rest - part.astype(f32)

    def over_kinds(line, part):
        terms = raw[line * each : (line + 1) * each] * factors[part]
        total = terms[0:parents]
        for which in range(1, each // parents):
            total = total + terms[which * parents : (which + 1) * parents]
        return total

    moved = [over_kinds(pol, 0) - over_kinds(pols + pol, 1) for pol in range(pols)]
    moved += [over_kinds(pol, 1) + over_kinds(pols + pol, 0) for pol in range(pols)]
    value = jnp.concatenate(moved, axis=0)
    for share in range(shares):
        out[share * height : (share + 1) * height, :] = value


def near_kernel(neighbours, near_count, low, current, high, blocks, out, padded):
    slots, boxes = neighbours.shape
    first = lax.axis_index("box") * boxes - boxes
    for part in range(2):
        padded[part, 0:boxes, :] = low[part]
        padded[part, boxes : 2 * boxes, :] = current[part]
        padded[part, 2 * boxes : 3 * boxes, :] = high[part]
        padded[part, 3 * boxes :, :] = jnp.zeros((8, 128), f32)
    for box in range(boxes):
        used = near_count[box]
        sum_re = jnp.zeros(out.shape[2:], f32)
        sum_im = jnp.zeros(out.shape[2:], f32)
        for slot in range(slots):
            at = jnp.where(slot < used, neighbours[slot, box] - first, 3 * boxes)
            cur_re, cur_im = padded[0, pl.ds(at, 1), :], padded[1, pl.ds(at, 1), :]
            block_re, block_im = blocks[0, box, slot], blocks[1, box, slot]
            sum_re = sum_re + (block_re * cur_re - block_im * cur_im)
            sum_im = sum_im + (block_re * cur_im + block_im * cur_re)
        out[0, box] = sum_re
        out[1, box] = sum_im


def field_kernel(shares, total, received, gathered, radiation, near, out, samples, rows, down):
    pols, boxes, own, width = radiation.shape[1:]
    piece = width // shares
    height = received.shape[0] // shares
    half, tall = height // 2, down.shape[0] // 2
    stride = gathered.shape[0] // total
    lanes = received.shape[1]

    def table_row(number):
        return number % total * stride + height + number // total

    def octants(number):
        ends = [number]
        for one in range(number + 1, number + 8):
            if one % total == 0:
                ends.append(one)
        ends.append(number + 8)
        parts = []
        for low, high in zip(ends[:-1], ends[1:]):
            if high - low == 1:
                parts.append(gathered[table_row(low) : table_row(low) + 1, :])
            else:
                parts.append(gathered[pl.ds(table_row(low), high - low, stride=stride), :])
        return parts[0] if len(parts) == 1 else jnp.concatenate(parts, axis=0)

    samples[...] = jnp.zeros_like(samples)
    sample = lax.broadcasted_iota(jnp.int32, (40, lanes), 0)
    offset = sample - lax.broadcasted_iota(jnp.int32, (40, lanes), 1) // (lanes // piece)
    contract = (((1,), (1,)), ((), ()))
    for share in range(shares):
        number = share * (16 + reach)
        shift_re, shift_im = octants(number), octants(number + 8)
        table = jnp.zeros((40, lanes), f32)
        for step in range(reach):
            at = table_row(number + 16 + step)
            table = jnp.where(offset == step, gathered[at : at + 1, :], table)
        for line in range(half):
            at = share * height + line
            moved_re, moved_im = received[at : at + 1, :], received[at + half : at + half + 1, :]
            down[line * 8 : line * 8 + 8, :] = moved_re * shift_re + moved_im * shift_im
            down[tall + line * 8 : tall + line * 8 + 8, :] = moved_im * shift_re - moved_re * shift_im
        value = down[...]
        value_hi = value.astype(jnp.bfloat16)
        value_lo = (value - value_hi.astype(f32)).astype(jnp.bfloat16)
        table_hi = table.astype(jnp.bfloat16)
        table_lo = (table - table_hi.astype(f32)).astype(jnp.bfloat16)
        settled = lax.dot_general(
            jnp.concatenate([table_hi, table_hi], axis=1),
            jnp.concatenate([value_hi, value_lo], axis=1),
            contract,
            preferred_element_type=f32,
        ) + lax.dot_general(table_lo, value_hi, contract, preferred_element_type=f32)
        first = lead - below + share * piece
        samples[first : first + 40, :] += settled
    samples[lead + width - below : lead + width, :] += samples[lead - below : lead, :]
    samples[lead : lead + above, :] += samples[lead + width : lead + width + above, :]
    for block in range(width // 128):
        rows[:, block * 128 : block * 128 + 128] = samples[lead + block * 128 : lead + block * 128 + 128, :].T
    lane = lax.broadcasted_iota(jnp.int32, (own, boxes), 1)
    all_re = jnp.zeros((own, boxes), f32)
    all_im = jnp.zeros((own, boxes), f32)
    for box in range(boxes):
        sum_re, sum_im = near[0, box], near[1, box]
        for pol in range(pols):
            at_re, at_im = pol * boxes + box, (pols + pol) * boxes + box
            for block in range(width // 128):
                cut = slice(block * 128, block * 128 + 128)
                in_re, in_im = rows[at_re : at_re + 1, cut], rows[at_im : at_im + 1, cut]
                rad_re, rad_im = radiation[0, pol, box, :, cut], radiation[1, pol, box, :, cut]
                sum_re = sum_re + (rad_re * in_re + rad_im * in_im)
                sum_im = sum_im + (rad_re * in_im - rad_im * in_re)
        all_re = jnp.where(lane == box, jnp.sum(sum_re, axis=1, keepdims=True), all_re)
        all_im = jnp.where(lane == box, jnp.sum(sum_im, axis=1, keepdims=True), all_im)
    out[0] = all_re
    out[1] = all_im


def local(
    current,
    near_block,
    neighbours,
    near_count,
    radiation,
    stencil,
    stencil_weight,
    child_shift,
    list_source,
    list_kind,
    list_count,
    translation,
):
    box_total, dir_total = lax.axis_size("box"), lax.axis_size("dir")
    _, pols, boxes, own, width = radiation.shape
    share = stencil.shape[0]
    parents = boxes // 8
    piece = width // dir_total
    span = piece + below + above
    lanes = 2 * pols * boxes
    held = lead + width + 8
    cuts = 4
    spare = -(-(16 + reach) // box_total)
    height = lanes // 8 + (16 + reach) * dir_total // box_total

    def shape(dims, dtype=f32):
        return jax.ShapeDtypeStruct(dims, dtype)

    forward = [(i, i + 1) for i in range(box_total - 1)]
    low = lax.ppermute(current, "box", forward)
    high = lax.ppermute(current, "box", [(b, a) for a, b in forward])

    windows = pl.pallas_call(
        functools.partial(leaf_kernel, cuts, dir_total, box_total, spare),
        out_shape=shape((dir_total * (span + spare), lanes)),
        in_specs=[HBM] * 5,
        out_specs=VMEM,
        scratch_shapes=[
            pltpu.VMEM(radiation.shape, f32),
            pltpu.VMEM(current.shape, f32),
            pltpu.VMEM((stencil.shape[1], share), jnp.int32),
            pltpu.VMEM((stencil.shape[1], share), f32),
            pltpu.VMEM(child_shift.shape, f32),
            pltpu.VMEM((spare * box_total + 16 + reach, share), f32),
            pltpu.VMEM((2, current.shape[2], boxes), f32),
            pltpu.VMEM((lanes, width), f32),
            pltpu.VMEM((held, lanes), f32),
            pltpu.SemaphoreType.DMA((cuts + 4,)),
        ],
        compiler_params=alone,
        name="leaf",
    )(current, stencil.T, stencil_weight.T, child_shift, radiation)
    windows = lax.all_to_all(windows.reshape(dir_total, 1, (span + spare) * lanes), "dir", 0, 0, tiled=True)

    kinds, tops_total = translation.shape[1], list_source.shape[0]
    interp, picks, factors = pl.pallas_call(
        functools.partial(plan_kernel, parents, width, piece),
        out_shape=(
            shape((128, share)),
            shape((2 * pols * kinds * parents, box_total * lanes // 8), dtype=jnp.bfloat16),
            shape((2, kinds * parents, share)),
        ),
        in_specs=[VMEM] * 6,
        out_specs=(VMEM, VMEM, VMEM),
        scratch_shapes=[pltpu.VMEM((tops_total, list_source.shape[1]), f32)],
        compiler_params=params,
        cost_estimate=pl.CostEstimate(flops=2_000_000, bytes_accessed=2_000_000, transcendentals=0),
        name="plan",
    )(stencil.T, stencil_weight.T, list_source.T, list_kind.T, list_count.reshape(1, -1), translation)

    near = pl.pallas_call(
        near_kernel,
        out_shape=shape((2, boxes, own, 128)),
        in_specs=[SMEM, SMEM] + [VMEM] * 4,
        out_specs=VMEM,
        scratch_shapes=[pltpu.VMEM((2, 3 * boxes + 8, 128), f32)],
        compiler_params=params,
        cost_estimate=pl.CostEstimate(flops=4_000_000, bytes_accessed=4_000_000, transcendentals=0),
        name="near",
    )(neighbours.T, near_count, low, current, high, near_block)

    tops = pl.pallas_call(
        functools.partial(lift_kernel, dir_total, box_total, spare),
        out_shape=shape((box_total * height, share)),
        in_specs=[VMEM] * 3 + [ANY],
        out_specs=VMEM,
        scratch_shapes=[pltpu.VMEM((128, lanes), f32), pltpu.VMEM((height, share), f32)],
        compiler_params=params,
        name="lift",
    )(windows.reshape(dir_total * (span + spare), lanes), interp, child_shift, near)
    gathered = lax.all_to_all(tops.reshape(box_total, 1, height * share), "box", 0, 0, tiled=True)
    gathered = gathered.reshape(box_total * height, share)

    moved = pl.pallas_call(
        functools.partial(lower_kernel, dir_total, parents),
        out_shape=shape((dir_total * lanes // 8, share)),
        in_specs=[VMEM] * 3,
        out_specs=VMEM,
        scratch_shapes=[pltpu.VMEM((box_total * lanes // 8, share), f32)],
        compiler_params=params,
        name="lower",
    )(picks, factors, gathered)
    moved = lax.all_to_all(moved.reshape(dir_total, 1, lanes // 8 * share), "dir", 0, 0, tiled=True)

    field = pl.pallas_call(
        functools.partial(field_kernel, dir_total, box_total),
        out_shape=shape((2, own, boxes)),
        in_specs=[VMEM] * 4,
        out_specs=VMEM,
        scratch_shapes=[pltpu.VMEM((held, lanes), f32), pltpu.VMEM((lanes, width), f32), pltpu.VMEM((lanes, share), f32)],
        compiler_params=params,
        name="field",
    )(moved.reshape(dir_total * lanes // 8, share), gathered, radiation, near)
    return field.transpose(0, 2, 1)


def solution(mesh):
    return jax.shard_map(
        local,
        mesh=mesh,
        in_specs=(
            P(None, "box", None),
            P(None, "box", None, "dir", None),
            P("box", None),
            P("box"),
            P(None, None, "box", "dir", None),
            P("dir", None),
            P("dir", None),
            P(None, None, "dir"),
            P(),
            P(),
            P(),
            P(None, None, "dir"),
        ),
        out_specs=P(None, "box", "dir"),
        check_vma=False,
    )
```

```python
import functools

import jax
import jax.numpy as jnp
from jax import lax
from jax.experimental import pallas as pl
from jax.experimental.pallas import tpu as pltpu
from jax.sharding import PartitionSpec as P

highest = lax.Precision.HIGHEST
f32 = jnp.float32
below, above = 1, 2
lead = 8
reach = below + above + 1
VMEM = pl.BlockSpec(memory_space=pltpu.VMEM)
SMEM = pl.BlockSpec(memory_space=pltpu.SMEM)
ANY = pl.BlockSpec(memory_space=pl.ANY)
HBM = pl.BlockSpec(memory_space=pltpu.HBM)
params = pltpu.CompilerParams(vmem_limit_bytes=12 * 2**20)
alone = pltpu.CompilerParams(vmem_limit_bytes=60 * 2**20)


def sums_of_eight(tiles):
    row = lax.broadcasted_iota(jnp.int32, tiles[0].shape, 0)
    for step in (1, 2, 4):
        even = (row & step) == 0
        tiles = [
            jnp.where(even, a, b) + pltpu.roll(jnp.where(even, b, a), 8 - step, 0)
            for a, b in zip(tiles[0::2], tiles[1::2])
        ]
    return tiles[0]


def leaf_kernel(cuts, shares, total, spare, current, stencil, weight, shift, radiation, out, patterns, *scratch):
    given, points, weights, shifts, tables, columns, rows, samples, sems = scratch
    pols, boxes, own, width = radiation.shape[1:]
    step = boxes // cuts
    small = [
        pltpu.make_async_copy(source, target, sems.at[cuts + index])
        for index, (source, target) in enumerate(((current, given), (stencil, points), (weight, weights), (shift, shifts)))
    ]
    for copy in small:
        copy.start()
    copies = []
    for cut in range(cuts):
        part = pl.ds(cut * step, step)
        copy = pltpu.make_async_copy(radiation.at[:, :, part], patterns.at[:, :, part], sems.at[cut])
        copy.start()
        copies.append(copy)
    for copy in small:
        copy.wait()
    for part in range(2):
        columns[part] = given[part].T
    place = lax.axis_index("dir")
    mine = pl.ds(pl.multiple_of(place * own, own), own)
    piece = width // shares
    lanes = stencil.shape[1]
    tables[0:8, :] = shifts[0]
    tables[8:16, :] = shifts[1]
    tables[16:, :] = jnp.zeros((tables.shape[0] - 16, lanes), f32)
    centre = place * piece - below + lax.broadcasted_iota(jnp.int32, (1, lanes), 1) // (lanes // piece)
    for offset in range(reach):
        line = jnp.zeros((1, lanes), f32)
        for point in range(stencil.shape[0]):
            at = lax.rem(points[point : point + 1, :] - centre + width, width)
            line = line + jnp.where(at == offset, weights[point : point + 1, :], 0.0)
        tables[16 + offset : 17 + offset, :] = line
    begin = lax.rem(lax.axis_index("box") + total - lax.rem(place * (16 + reach), total), total)
    real, imag = columns[0, mine, :], columns[1, mine, :]
    for cut in range(cuts):
        copies[cut].wait()
        for group in range(cut * step, (cut + 1) * step, 8):
            eight = range(group, group + 8)
            cur_re = [jnp.broadcast_to(real[:, box : box + 1], (own, 128)) for box in eight]
            cur_im = [jnp.broadcast_to(imag[:, box : box + 1], (own, 128)) for box in eight]
            for pol in range(pols):
                for block in range(width // 128):
                    at = slice(block * 128, block * 128 + 128)
                    rad_re = [patterns[0, pol, box, :, at] for box in eight]
                    rad_im = [patterns[1, pol, box, :, at] for box in eight]
                    both = list(zip(rad_re, rad_im, cur_re, cur_im))
                    line = pol * boxes + group
                    rows[line : line + 8, at] = sums_of_eight([a * c - b * d for a, b, c, d in both])
                    line = (pols + pol) * boxes + group
                    rows[line : line + 8, at] = sums_of_eight([a * d + b * c for a, b, c, d in both])
    for block in range(width // 128):
        samples[lead + block * 128 : lead + block * 128 + 128, :] = rows[:, block * 128 : block * 128 + 128].T
    samples[lead - below : lead, :] = samples[lead + width - below : lead + width, :]
    samples[lead + width : lead + width + above, :] = samples[lead : lead + above, :]
    span = piece + below + above
    own_rows = [tables[pl.ds(begin + index * total, 1), :] for index in range(spare)]
    for share in range(shares):
        first, at = lead - below + share * piece, share * (span + spare)
        out[at : at + span, :] = samples[first : first + span, :]
        for index in range(spare):
            out[at + span + index : at + span + index + 1, :] = own_rows[index]


def plan_kernel(parents, width, piece, stencil, weight, source, kind, count, translation, interp, picks, factors, codes):
    lanes = stencil.shape[1]
    begin = lax.axis_index("dir") * piece - below
    row = lax.broadcasted_iota(jnp.int32, (128, lanes), 0)
    table = jnp.zeros((128, lanes), f32)
    for point in range(stencil.shape[0]):
        at = lax.rem(stencil[point : point + 1, :] - begin + width, width)
        table = table + jnp.where(row == at, weight[point : point + 1, :], 0.0)
    interp[...] = table
    kinds = translation.shape[1]
    slots, tops = source.shape
    lines, columns = picks.shape[0] // (kinds * parents), picks.shape[1]
    origin = source[...]
    spot = (origin // parents) * (lines * parents) + lax.rem(origin, parents)
    live = lax.broadcasted_iota(jnp.int32, (slots, tops), 0) < count[...]
    codes[...] = jnp.where(live, kind[...] * columns + spot, -1).astype(f32).T
    mine = codes[pl.ds(lax.axis_index("box") * parents, parents), :]
    own_kind = lax.broadcasted_iota(jnp.int32, (kinds * parents, slots), 0) // parents
    mine = jnp.concatenate([mine] * kinds, axis=0) - (own_kind * columns).astype(f32)
    lane = lax.broadcasted_iota(jnp.int32, (kinds * parents, columns), 1).astype(f32)
    counts = jnp.zeros((kinds * parents, columns), f32)
    for slot in range(slots):
        counts = counts + jnp.where(mine[:, slot : slot + 1] == lane, 1.0, 0.0)
    parts = [pltpu.roll(counts, line * parents, 1) if line else counts for line in range(lines)]
    picks[...] = jnp.concatenate(parts, axis=0).astype(jnp.bfloat16)
    for part in range(2):
        for which in range(kinds):
            one = translation[part, which : which + 1, :]
            factors[part, which * parents : (which + 1) * parents, :] = jnp.broadcast_to(one, (parents, lanes))


def lift_kernel(shares, copies, spare, received, interp, shift, near, out, total, tops):
    each = received.shape[0] // shares
    span = each - spare
    total[...] = jnp.zeros_like(total)
    part = received[0:span, :]
    for share in range(1, shares):
        part = part + received[share * each : share * each + span, :]
    total[0:span, :] = part
    up = jnp.dot(total[...].T, interp[...], precision=highest, preferred_element_type=f32)
    shift_re, shift_im = shift[0], shift[1]
    half = up.shape[0] // 2
    lines = half // 8
    for line in range(lines):
        up_re, up_im = up[line * 8 : line * 8 + 8], up[half + line * 8 : half + line * 8 + 8]
        tops[line : line + 1, :] = jnp.sum(up_re * shift_re - up_im * shift_im, axis=0, keepdims=True)
        tops[lines + line : lines + line + 1, :] = jnp.sum(up_re * shift_im + up_im * shift_re, axis=0, keepdims=True)
    height = tops.shape[0]
    place = lax.axis_index("box")
    for index in range(height - 2 * lines):
        number = place + index * copies
        share = number // (16 + reach)
        at = share * each + span + (number - share * (16 + reach)) // copies
        tops[2 * lines + index : 2 * lines + index + 1, :] = received[pl.ds(at, 1), :]
    value = tops[...]
    for copy in range(copies):
        out[copy * height : (copy + 1) * height, :] = value


def lower_kernel(shares, parents, picks, factors, gathered, out, compact):
    each = factors.shape[1]
    lines = picks.shape[0] // each
    pols = lines // 2
    height = lines * parents
    boxes = compact.shape[0] // height
    stride = gathered.shape[0] // boxes
    for box in range(boxes):
        compact[box * height : (box + 1) * height, :] = gathered[box * stride : box * stride + height, :]
    rest = compact[...]
    table = picks[...]
    raw = jnp.zeros((table.shape[0], rest.shape[1]), f32)
    for _ in range(3):
        part = rest.astype(jnp.bfloat16)
        raw = raw + jnp.dot(table, part, preferred_element_type=f32)
        rest = rest - part.astype(f32)

    def over_kinds(line, part):
        terms = raw[line * each : (line + 1) * each] * factors[part]
        total = terms[0:parents]
        for which in range(1, each // parents):
            total = total + terms[which * parents : (which + 1) * parents]
        return total

    moved = [over_kinds(pol, 0) - over_kinds(pols + pol, 1) for pol in range(pols)]
    moved += [over_kinds(pol, 1) + over_kinds(pols + pol, 0) for pol in range(pols)]
    value = jnp.concatenate(moved, axis=0)
    for share in range(shares):
        out[share * height : (share + 1) * height, :] = value


def near_kernel(neighbours, near_count, low, current, high, blocks, out, padded):
    slots, boxes = neighbours.shape
    first = lax.axis_index("box") * boxes - boxes
    for part in range(2):
        padded[part, 0:boxes, :] = low[part]
        padded[part, boxes : 2 * boxes, :] = current[part]
        padded[part, 2 * boxes : 3 * boxes, :] = high[part]
        padded[part, 3 * boxes :, :] = jnp.zeros((8, 128), f32)
    for box in range(boxes):
        used = near_count[box]
        sum_re = jnp.zeros(out.shape[2:], f32)
        sum_im = jnp.zeros(out.shape[2:], f32)
        for slot in range(slots):
            at = jnp.where(slot < used, neighbours[slot, box] - first, 3 * boxes)
            cur_re, cur_im = padded[0, pl.ds(at, 1), :], padded[1, pl.ds(at, 1), :]
            block_re, block_im = blocks[0, box, slot], blocks[1, box, slot]
            sum_re = sum_re + (block_re * cur_re - block_im * cur_im)
            sum_im = sum_im + (block_re * cur_im + block_im * cur_re)
        out[0, box] = sum_re
        out[1, box] = sum_im


def field_kernel(shares, total, received, gathered, radiation, near, out, samples, rows, down):
    pols, boxes, own, width = radiation.shape[1:]
    piece = width // shares
    height = received.shape[0] // shares
    half, tall = height // 2, down.shape[0] // 2
    stride = gathered.shape[0] // total
    lanes = received.shape[1]

    def table_row(number):
        return number % total * stride + height + number // total

    def octants(number):
        ends = [number]
        for one in range(number + 1, number + 8):
            if one % total == 0:
                ends.append(one)
        ends.append(number + 8)
        parts = []
        for low, high in zip(ends[:-1], ends[1:]):
            if high - low == 1:
                parts.append(gathered[table_row(low) : table_row(low) + 1, :])
            else:
                parts.append(gathered[pl.ds(table_row(low), high - low, stride=stride), :])
        return parts[0] if len(parts) == 1 else jnp.concatenate(parts, axis=0)

    samples[...] = jnp.zeros_like(samples)
    sample = lax.broadcasted_iota(jnp.int32, (40, lanes), 0)
    offset = sample - lax.broadcasted_iota(jnp.int32, (40, lanes), 1) // (lanes // piece)
    contract = (((1,), (1,)), ((), ()))
    for share in range(shares):
        number = share * (16 + reach)
        shift_re, shift_im = octants(number), octants(number + 8)
        table = jnp.zeros((40, lanes), f32)
        for step in range(reach):
            at = table_row(number + 16 + step)
            table = jnp.where(offset == step, gathered[at : at + 1, :], table)
        for line in range(half):
            at = share * height + line
            moved_re, moved_im = received[at : at + 1, :], received[at + half : at + half + 1, :]
            down[line * 8 : line * 8 + 8, :] = moved_re * shift_re + moved_im * shift_im
            down[tall + line * 8 : tall + line * 8 + 8, :] = moved_im * shift_re - moved_re * shift_im
        value = down[...]
        value_hi = value.astype(jnp.bfloat16)
        value_lo = (value - value_hi.astype(f32)).astype(jnp.bfloat16)
        table_hi = table.astype(jnp.bfloat16)
        table_lo = (table - table_hi.astype(f32)).astype(jnp.bfloat16)
        settled = lax.dot_general(
            jnp.concatenate([table_hi, table_hi], axis=1),
            jnp.concatenate([value_hi, value_lo], axis=1),
            contract,
            preferred_element_type=f32,
        ) + lax.dot_general(table_lo, value_hi, contract, preferred_element_type=f32)
        first = lead - below + share * piece
        samples[first : first + 40, :] += settled
    samples[lead + width - below : lead + width, :] += samples[lead - below : lead, :]
    samples[lead : lead + above, :] += samples[lead + width : lead + width + above, :]
    for block in range(width // 128):
        rows[:, block * 128 : block * 128 + 128] = samples[lead + block * 128 : lead + block * 128 + 128, :].T
    lane = lax.broadcasted_iota(jnp.int32, (own, boxes), 1)
    all_re = jnp.zeros((own, boxes), f32)
    all_im = jnp.zeros((own, boxes), f32)
    for box in range(boxes):
        sum_re, sum_im = near[0, box], near[1, box]
        for pol in range(pols):
            at_re, at_im = pol * boxes + box, (pols + pol) * boxes + box
            for block in range(width // 128):
                cut = slice(block * 128, block * 128 + 128)
                in_re, in_im = rows[at_re : at_re + 1, cut], rows[at_im : at_im + 1, cut]
                rad_re, rad_im = radiation[0, pol, box, :, cut], radiation[1, pol, box, :, cut]
                sum_re = sum_re + (rad_re * in_re + rad_im * in_im)
                sum_im = sum_im + (rad_re * in_im - rad_im * in_re)
        all_re = jnp.where(lane == box, jnp.sum(sum_re, axis=1, keepdims=True), all_re)
        all_im = jnp.where(lane == box, jnp.sum(sum_im, axis=1, keepdims=True), all_im)
    out[0] = all_re
    out[1] = all_im


def local(
    current,
    near_block,
    neighbours,
    near_count,
    radiation,
    stencil,
    stencil_weight,
    child_shift,
    list_source,
    list_kind,
    list_count,
    translation,
):
    box_total, dir_total = lax.axis_size("box"), lax.axis_size("dir")
    _, pols, boxes, own, width = radiation.shape
    share = stencil.shape[0]
    parents = boxes // 8
    piece = width // dir_total
    span = piece + below + above
    lanes = 2 * pols * boxes
    held = lead + width + 8
    cuts = 4
    spare = -(-(16 + reach) // box_total)
    height = lanes // 8 + (16 + reach) * dir_total // box_total

    def shape(dims, dtype=f32):
        return jax.ShapeDtypeStruct(dims, dtype)

    forward = [(i, i + 1) for i in range(box_total - 1)]
    low = lax.ppermute(current, "box", forward)
    high = lax.ppermute(current, "box", [(b, a) for a, b in forward])

    windows = pl.pallas_call(
        functools.partial(leaf_kernel, cuts, dir_total, box_total, spare),
        out_shape=shape((dir_total * (span + spare), lanes)),
        in_specs=[HBM] * 5,
        out_specs=VMEM,
        scratch_shapes=[
            pltpu.VMEM(radiation.shape, f32),
            pltpu.VMEM(current.shape, f32),
            pltpu.VMEM((stencil.shape[1], share), jnp.int32),
            pltpu.VMEM((stencil.shape[1], share), f32),
            pltpu.VMEM(child_shift.shape, f32),
            pltpu.VMEM((spare * box_total + 16 + reach, share), f32),
            pltpu.VMEM((2, current.shape[2], boxes), f32),
            pltpu.VMEM((lanes, width), f32),
            pltpu.VMEM((held, lanes), f32),
            pltpu.SemaphoreType.DMA((cuts + 4,)),
        ],
        compiler_params=alone,
        name="leaf",
    )(current, stencil.T, stencil_weight.T, child_shift, radiation)
    windows = lax.all_to_all(windows.reshape(dir_total, 1, (span + spare) * lanes), "dir", 0, 0, tiled=True)

    kinds, tops_total = translation.shape[1], list_source.shape[0]
    interp, picks, factors = pl.pallas_call(
        functools.partial(plan_kernel, parents, width, piece),
        out_shape=(
            shape((128, share)),
            shape((2 * pols * kinds * parents, box_total * lanes // 8), dtype=jnp.bfloat16),
            shape((2, kinds * parents, share)),
        ),
        in_specs=[VMEM] * 6,
        out_specs=(VMEM, VMEM, VMEM),
        scratch_shapes=[pltpu.VMEM((tops_total, list_source.shape[1]), f32)],
        compiler_params=params,
        cost_estimate=pl.CostEstimate(flops=2_000_000, bytes_accessed=2_000_000, transcendentals=0),
        name="plan",
    )(stencil.T, stencil_weight.T, list_source.T, list_kind.T, list_count.reshape(1, -1), translation)

    near = pl.pallas_call(
        near_kernel,
        out_shape=shape((2, boxes, own, 128)),
        in_specs=[SMEM, SMEM] + [VMEM] * 4,
        out_specs=VMEM,
        scratch_shapes=[pltpu.VMEM((2, 3 * boxes + 8, 128), f32)],
        compiler_params=params,
        cost_estimate=pl.CostEstimate(flops=4_000_000, bytes_accessed=4_000_000, transcendentals=0),
        name="near",
    )(neighbours.T, near_count, low, current, high, near_block)

    tops = pl.pallas_call(
        functools.partial(lift_kernel, dir_total, box_total, spare),
        out_shape=shape((box_total * height, share)),
        in_specs=[VMEM] * 3 + [ANY],
        out_specs=VMEM,
        scratch_shapes=[pltpu.VMEM((128, lanes), f32), pltpu.VMEM((height, share), f32)],
        compiler_params=params,
        name="lift",
    )(windows.reshape(dir_total * (span + spare), lanes), interp, child_shift, near)
    gathered = lax.all_to_all(tops.reshape(box_total, 1, height * share), "box", 0, 0, tiled=True)
    gathered = gathered.reshape(box_total * height, share)

    moved = pl.pallas_call(
        functools.partial(lower_kernel, dir_total, parents),
        out_shape=shape((dir_total * lanes // 8, share)),
        in_specs=[VMEM] * 3,
        out_specs=VMEM,
        scratch_shapes=[pltpu.VMEM((box_total * lanes // 8, share), f32)],
        compiler_params=params,
        name="lower",
    )(picks, factors, gathered)
    moved = lax.all_to_all(moved.reshape(dir_total, 1, lanes // 8 * share), "dir", 0, 0, tiled=True)

    field = pl.pallas_call(
        functools.partial(field_kernel, dir_total, box_total),
        out_shape=shape((2, own, boxes)),
        in_specs=[VMEM] * 4,
        out_specs=VMEM,
        scratch_shapes=[pltpu.VMEM((held, lanes), f32), pltpu.VMEM((lanes, width), f32), pltpu.VMEM((lanes, share), f32)],
        compiler_params=params,
        name="field",
    )(moved.reshape(dir_total * lanes // 8, share), gathered, radiation, near)
    return field.transpose(0, 2, 1)


def solution(mesh):
    return jax.shard_map(
        local,
        mesh=mesh,
        in_specs=(
            P(None, "box", None),
            P(None, "box", None, "dir", None),
            P("box", None),
            P("box"),
            P(None, None, "box", "dir", None),
            P("dir", None),
            P("dir", None),
            P(None, None, "dir"),
            P(),
            P(),
            P(),
            P(None, None, "dir"),
        ),
        out_specs=P(None, "box", "dir"),
        check_vma=False,
    )
```

```python
import functools

import jax
import jax.numpy as jnp
from jax import lax
from jax.experimental import pallas as pl
from jax.experimental.pallas import tpu as pltpu
from jax.sharding import PartitionSpec as P

highest = lax.Precision.HIGHEST
f32 = jnp.float32
below, above = 1, 2
lead = 8
tall_window = 48
reach = below + above + 1
VMEM = pl.BlockSpec(memory_space=pltpu.VMEM)
SMEM = pl.BlockSpec(memory_space=pltpu.SMEM)
ANY = pl.BlockSpec(memory_space=pl.ANY)
HBM = pl.BlockSpec(memory_space=pltpu.HBM)
params = pltpu.CompilerParams(vmem_limit_bytes=12 * 2**20)
alone = pltpu.CompilerParams(vmem_limit_bytes=60 * 2**20)


def sums_of_eight(tiles):
    row = lax.broadcasted_iota(jnp.int32, tiles[0].shape, 0)
    for step in (1, 2, 4):
        even = (row & step) == 0
        tiles = [
            jnp.where(even, a, b) + pltpu.roll(jnp.where(even, b, a), 8 - step, 0)
            for a, b in zip(tiles[0::2], tiles[1::2])
        ]
    return tiles[0]


def leaf_kernel(cuts, shares, total, spare, current, stencil, weight, shift, radiation, out, patterns, *scratch):
    given, points, weights, shifts, tables, columns, rows, samples, sems = scratch
    pols, boxes, own, width = radiation.shape[1:]
    step = boxes // cuts
    small = [
        pltpu.make_async_copy(source, target, sems.at[cuts + index])
        for index, (source, target) in enumerate(((current, given), (stencil, points), (weight, weights), (shift, shifts)))
    ]
    for copy in small:
        copy.start()
    copies = []
    for cut in range(cuts):
        part = pl.ds(cut * step, step)
        copy = pltpu.make_async_copy(radiation.at[:, :, part], patterns.at[:, :, part], sems.at[cut])
        copy.start()
        copies.append(copy)
    for copy in small:
        copy.wait()
    for part in range(2):
        columns[part] = given[part].T
    place = lax.axis_index("dir")
    mine = pl.ds(pl.multiple_of(place * own, own), own)
    piece = width // shares
    lanes = stencil.shape[1]
    tables[0:8, :] = shifts[0]
    tables[8:16, :] = shifts[1]
    tables[16:, :] = jnp.zeros((tables.shape[0] - 16, lanes), f32)
    centre = place * piece - below + lax.broadcasted_iota(jnp.int32, (1, lanes), 1) // (lanes // piece)
    for offset in range(reach):
        line = jnp.zeros((1, lanes), f32)
        for point in range(stencil.shape[0]):
            at = lax.rem(points[point : point + 1, :] - centre + width, width)
            line = line + jnp.where(at == offset, weights[point : point + 1, :], 0.0)
        tables[16 + offset : 17 + offset, :] = line
    begin = lax.rem(lax.axis_index("box") + total - lax.rem(place * (16 + reach), total), total)
    real, imag = columns[0, mine, :], columns[1, mine, :]
    for cut in range(cuts):
        copies[cut].wait()
        for group in range(cut * step, (cut + 1) * step, 8):
            eight = range(group, group + 8)
            cur_re = [jnp.broadcast_to(real[:, box : box + 1], (own, 128)) for box in eight]
            cur_im = [jnp.broadcast_to(imag[:, box : box + 1], (own, 128)) for box in eight]
            for pol in range(pols):
                for block in range(width // 128):
                    at = slice(block * 128, block * 128 + 128)
                    rad_re = [patterns[0, pol, box, :, at] for box in eight]
                    rad_im = [patterns[1, pol, box, :, at] for box in eight]
                    both = list(zip(rad_re, rad_im, cur_re, cur_im))
                    line = pol * boxes + group
                    rows[line : line + 8, at] = sums_of_eight([a * c - b * d for a, b, c, d in both])
                    line = (pols + pol) * boxes + group
                    rows[line : line + 8, at] = sums_of_eight([a * d + b * c for a, b, c, d in both])
    for block in range(width // 128):
        samples[lead + block * 128 : lead + block * 128 + 128, :] = rows[:, block * 128 : block * 128 + 128].T
    samples[lead - below : lead, :] = samples[lead + width - below : lead + width, :]
    samples[lead + width : lead + width + above, :] = samples[lead : lead + above, :]
    span = piece + below + above
    own_rows = [tables[pl.ds(begin + index * total, 1), :] for index in range(spare)]
    for share in range(shares):
        first, at = lead - below + share * piece, share * (span + spare)
        out[at : at + span, :] = samples[first : first + span, :]
        for index in range(spare):
            out[at + span + index : at + span + index + 1, :] = own_rows[index]


def plan_kernel(parents, width, piece, stencil, weight, source, kind, count, translation, interp, picks, factors, codes):
    lanes = stencil.shape[1]
    begin = lax.axis_index("dir") * piece - below
    row = lax.broadcasted_iota(jnp.int32, (128, lanes), 0)
    table = jnp.zeros((128, lanes), f32)
    for point in range(stencil.shape[0]):
        at = lax.rem(stencil[point : point + 1, :] - begin + width, width)
        table = table + jnp.where(row == at, weight[point : point + 1, :], 0.0)
    interp[...] = table
    kinds = translation.shape[1]
    slots, tops = source.shape
    lines, columns = picks.shape[0] // (kinds * parents), picks.shape[1]
    origin = source[...]
    spot = (origin // parents) * (lines * parents) + lax.rem(origin, parents)
    live = lax.broadcasted_iota(jnp.int32, (slots, tops), 0) < count[...]
    codes[...] = jnp.where(live, kind[...] * columns + spot, -1).astype(f32).T
    mine = codes[pl.ds(lax.axis_index("box") * parents, parents), :]
    own_kind = lax.broadcasted_iota(jnp.int32, (kinds * parents, slots), 0) // parents
    mine = jnp.concatenate([mine] * kinds, axis=0) - (own_kind * columns).astype(f32)
    lane = lax.broadcasted_iota(jnp.int32, (kinds * parents, columns), 1).astype(f32)
    counts = jnp.zeros((kinds * parents, columns), f32)
    for slot in range(slots):
        counts = counts + jnp.where(mine[:, slot : slot + 1] == lane, 1.0, 0.0)
    parts = [pltpu.roll(counts, line * parents, 1) if line else counts for line in range(lines)]
    picks[...] = jnp.concatenate(parts, axis=0).astype(jnp.bfloat16)
    for part in range(2):
        for which in range(kinds):
            one = translation[part, which : which + 1, :]
            factors[part, which * parents : (which + 1) * parents, :] = jnp.broadcast_to(one, (parents, lanes))


def lift_kernel(shares, copies, spare, received, interp, shift, near, out, total, tops):
    each = received.shape[0] // shares
    span = each - spare
    total[...] = jnp.zeros_like(total)
    part = received[0:span, :]
    for share in range(1, shares):
        part = part + received[share * each : share * each + span, :]
    total[0:span, :] = part
    up = jnp.dot(total[...].T, interp[...], precision=highest, preferred_element_type=f32)
    shift_re, shift_im = shift[0], shift[1]
    half = up.shape[0] // 2
    lines = half // 8
    for line in range(lines):
        up_re, up_im = up[line * 8 : line * 8 + 8], up[half + line * 8 : half + line * 8 + 8]
        tops[line : line + 1, :] = jnp.sum(up_re * shift_re - up_im * shift_im, axis=0, keepdims=True)
        tops[lines + line : lines + line + 1, :] = jnp.sum(up_re * shift_im + up_im * shift_re, axis=0, keepdims=True)
    height = tops.shape[0]
    place = lax.axis_index("box")
    for index in range(height - 2 * lines):
        number = place + index * copies
        share = number // (16 + reach)
        at = share * each + span + (number - share * (16 + reach)) // copies
        tops[2 * lines + index : 2 * lines + index + 1, :] = received[pl.ds(at, 1), :]
    value = tops[...]
    for copy in range(copies):
        out[copy * height : (copy + 1) * height, :] = value


def lower_kernel(shares, parents, picks, factors, gathered, out, compact):
    each = factors.shape[1]
    lines = picks.shape[0] // each
    pols = lines // 2
    height = lines * parents
    boxes = compact.shape[0] // height
    stride = gathered.shape[0] // boxes
    for box in range(boxes):
        compact[box * height : (box + 1) * height, :] = gathered[box * stride : box * stride + height, :]
    rest = compact[...]
    table = picks[...]
    raw = jnp.zeros((table.shape[0], rest.shape[1]), f32)
    for _ in range(3):
        part = rest.astype(jnp.bfloat16)
        raw = raw + jnp.dot(table, part, preferred_element_type=f32)
        rest = rest - part.astype(f32)

    def over_kinds(line, part):
        terms = raw[line * each : (line + 1) * each] * factors[part]
        total = terms[0:parents]
        for which in range(1, each // parents):
            total = total + terms[which * parents : (which + 1) * parents]
        return total

    moved = [over_kinds(pol, 0) - over_kinds(pols + pol, 1) for pol in range(pols)]
    moved += [over_kinds(pol, 1) + over_kinds(pols + pol, 0) for pol in range(pols)]
    value = jnp.concatenate(moved, axis=0)
    for share in range(shares):
        out[share * height : (share + 1) * height, :] = value


def near_kernel(neighbours, near_count, low, current, high, blocks, out, padded):
    slots, boxes = neighbours.shape
    first = lax.axis_index("box") * boxes - boxes
    for part in range(2):
        padded[part, 0:boxes, :] = low[part]
        padded[part, boxes : 2 * boxes, :] = current[part]
        padded[part, 2 * boxes : 3 * boxes, :] = high[part]
        padded[part, 3 * boxes :, :] = jnp.zeros((8, 128), f32)
    for box in range(boxes):
        used = near_count[box]
        sum_re = jnp.zeros(out.shape[2:], f32)
        sum_im = jnp.zeros(out.shape[2:], f32)
        for slot in range(slots):
            at = jnp.where(slot < used, neighbours[slot, box] - first, 3 * boxes)
            cur_re, cur_im = padded[0, pl.ds(at, 1), :], padded[1, pl.ds(at, 1), :]
            block_re, block_im = blocks[0, box, slot], blocks[1, box, slot]
            sum_re = sum_re + (block_re * cur_re - block_im * cur_im)
            sum_im = sum_im + (block_re * cur_im + block_im * cur_re)
        out[0, box] = sum_re
        out[1, box] = sum_im


def field_kernel(shares, total, received, gathered, radiation, near, out, samples, rows, down):
    pols, boxes, own, width = radiation.shape[1:]
    piece = width // shares
    height = received.shape[0] // shares
    half, tall = height // 2, down.shape[0] // 2
    stride = gathered.shape[0] // total
    lanes = received.shape[1]

    def table_row(number):
        return number % total * stride + height + number // total

    def octants(number):
        ends = [number]
        for one in range(number + 1, number + 8):
            if one % total == 0:
                ends.append(one)
        ends.append(number + 8)
        parts = []
        for low, high in zip(ends[:-1], ends[1:]):
            if high - low == 1:
                parts.append(gathered[table_row(low) : table_row(low) + 1, :])
            else:
                parts.append(gathered[pl.ds(table_row(low), high - low, stride=stride), :])
        return parts[0] if len(parts) == 1 else jnp.concatenate(parts, axis=0)

    samples[...] = jnp.zeros_like(samples)
    sample = lax.broadcasted_iota(jnp.int32, (tall_window, lanes), 0)
    offset = sample - lax.broadcasted_iota(jnp.int32, (tall_window, lanes), 1) // (lanes // piece)
    contract = (((1,), (1,)), ((), ()))
    for share in range(shares):
        number = share * (16 + reach)
        shift_re, shift_im = octants(number), octants(number + 8)
        table = jnp.zeros((tall_window, lanes), f32)
        for step in range(reach):
            at = table_row(number + 16 + step)
            table = jnp.where(offset == step, gathered[at : at + 1, :], table)
        for line in range(half):
            at = share * height + line
            moved_re, moved_im = received[at : at + 1, :], received[at + half : at + half + 1, :]
            down[line * 8 : line * 8 + 8, :] = moved_re * shift_re + moved_im * shift_im
            down[tall + line * 8 : tall + line * 8 + 8, :] = moved_im * shift_re - moved_re * shift_im
        value = down[...]
        value_hi = value.astype(jnp.bfloat16)
        value_lo = (value - value_hi.astype(f32)).astype(jnp.bfloat16)
        table_hi = table.astype(jnp.bfloat16)
        table_lo = (table - table_hi.astype(f32)).astype(jnp.bfloat16)
        tables = jnp.concatenate([table_hi, table_lo], axis=0)
        both = lax.dot_general(
            jnp.concatenate([tables, tables], axis=1),
            jnp.concatenate([value_hi, value_lo], axis=1),
            contract,
            preferred_element_type=f32,
        )
        settled = both[:tall_window] + both[tall_window:]
        first = lead - below + share * piece
        samples[first : first + tall_window, :] += settled
    samples[lead + width - below : lead + width, :] += samples[lead - below : lead, :]
    samples[lead : lead + above, :] += samples[lead + width : lead + width + above, :]
    for block in range(width // 128):
        rows[:, block * 128 : block * 128 + 128] = samples[lead + block * 128 : lead + block * 128 + 128, :].T
    lane = lax.broadcasted_iota(jnp.int32, (own, boxes), 1)
    all_re = jnp.zeros((own, boxes), f32)
    all_im = jnp.zeros((own, boxes), f32)
    for box in range(boxes):
        sum_re, sum_im = near[0, box], near[1, box]
        for pol in range(pols):
            at_re, at_im = pol * boxes + box, (pols + pol) * boxes + box
            for block in range(width // 128):
                cut = slice(block * 128, block * 128 + 128)
                in_re, in_im = rows[at_re : at_re + 1, cut], rows[at_im : at_im + 1, cut]
                rad_re, rad_im = radiation[0, pol, box, :, cut], radiation[1, pol, box, :, cut]
                sum_re = sum_re + (rad_re * in_re + rad_im * in_im)
                sum_im = sum_im + (rad_re * in_im - rad_im * in_re)
        all_re = jnp.where(lane == box, jnp.sum(sum_re, axis=1, keepdims=True), all_re)
        all_im = jnp.where(lane == box, jnp.sum(sum_im, axis=1, keepdims=True), all_im)
    out[0] = all_re
    out[1] = all_im


def local(
    current,
    near_block,
    neighbours,
    near_count,
    radiation,
    stencil,
    stencil_weight,
    child_shift,
    list_source,
    list_kind,
    list_count,
    translation,
):
    box_total, dir_total = lax.axis_size("box"), lax.axis_size("dir")
    _, pols, boxes, own, width = radiation.shape
    share = stencil.shape[0]
    parents = boxes // 8
    piece = width // dir_total
    span = piece + below + above
    lanes = 2 * pols * boxes
    held = lead + width + 16
    cuts = 4
    spare = -(-(16 + reach) // box_total)
    height = lanes // 8 + (16 + reach) * dir_total // box_total

    def shape(dims, dtype=f32):
        return jax.ShapeDtypeStruct(dims, dtype)

    forward = [(i, i + 1) for i in range(box_total - 1)]
    low = lax.ppermute(current, "box", forward)
    high = lax.ppermute(current, "box", [(b, a) for a, b in forward])

    windows = pl.pallas_call(
        functools.partial(leaf_kernel, cuts, dir_total, box_total, spare),
        out_shape=shape((dir_total * (span + spare), lanes)),
        in_specs=[HBM] * 5,
        out_specs=VMEM,
        scratch_shapes=[
            pltpu.VMEM(radiation.shape, f32),
            pltpu.VMEM(current.shape, f32),
            pltpu.VMEM((stencil.shape[1], share), jnp.int32),
            pltpu.VMEM((stencil.shape[1], share), f32),
            pltpu.VMEM(child_shift.shape, f32),
            pltpu.VMEM((spare * box_total + 16 + reach, share), f32),
            pltpu.VMEM((2, current.shape[2], boxes), f32),
            pltpu.VMEM((lanes, width), f32),
            pltpu.VMEM((held, lanes), f32),
            pltpu.SemaphoreType.DMA((cuts + 4,)),
        ],
        compiler_params=alone,
        name="leaf",
    )(current, stencil.T, stencil_weight.T, child_shift, radiation)
    windows = lax.all_to_all(windows.reshape(dir_total, 1, (span + spare) * lanes), "dir", 0, 0, tiled=True)

    kinds, tops_total = translation.shape[1], list_source.shape[0]
    interp, picks, factors = pl.pallas_call(
        functools.partial(plan_kernel, parents, width, piece),
        out_shape=(
            shape((128, share)),
            shape((2 * pols * kinds * parents, box_total * lanes // 8), dtype=jnp.bfloat16),
            shape((2, kinds * parents, share)),
        ),
        in_specs=[VMEM] * 6,
        out_specs=(VMEM, VMEM, VMEM),
        scratch_shapes=[pltpu.VMEM((tops_total, list_source.shape[1]), f32)],
        compiler_params=params,
        cost_estimate=pl.CostEstimate(flops=2_000_000, bytes_accessed=2_000_000, transcendentals=0),
        name="plan",
    )(stencil.T, stencil_weight.T, list_source.T, list_kind.T, list_count.reshape(1, -1), translation)

    near = pl.pallas_call(
        near_kernel,
        out_shape=shape((2, boxes, own, 128)),
        in_specs=[SMEM, SMEM] + [VMEM] * 4,
        out_specs=VMEM,
        scratch_shapes=[pltpu.VMEM((2, 3 * boxes + 8, 128), f32)],
        compiler_params=params,
        cost_estimate=pl.CostEstimate(flops=4_000_000, bytes_accessed=4_000_000, transcendentals=0),
        name="near",
    )(neighbours.T, near_count, low, current, high, near_block)

    tops = pl.pallas_call(
        functools.partial(lift_kernel, dir_total, box_total, spare),
        out_shape=shape((box_total * height, share)),
        in_specs=[VMEM] * 3 + [ANY],
        out_specs=VMEM,
        scratch_shapes=[pltpu.VMEM((128, lanes), f32), pltpu.VMEM((height, share), f32)],
        compiler_params=params,
        name="lift",
    )(windows.reshape(dir_total * (span + spare), lanes), interp, child_shift, near)
    gathered = lax.all_to_all(tops.reshape(box_total, 1, height * share), "box", 0, 0, tiled=True)
    gathered = gathered.reshape(box_total * height, share)

    moved = pl.pallas_call(
        functools.partial(lower_kernel, dir_total, parents),
        out_shape=shape((dir_total * lanes // 8, share)),
        in_specs=[VMEM] * 3,
        out_specs=VMEM,
        scratch_shapes=[pltpu.VMEM((box_total * lanes // 8, share), f32)],
        compiler_params=params,
        name="lower",
    )(picks, factors, gathered)
    moved = lax.all_to_all(moved.reshape(dir_total, 1, lanes // 8 * share), "dir", 0, 0, tiled=True)

    field = pl.pallas_call(
        functools.partial(field_kernel, dir_total, box_total),
        out_shape=shape((2, own, boxes)),
        in_specs=[VMEM] * 4,
        out_specs=VMEM,
        scratch_shapes=[pltpu.VMEM((held, lanes), f32), pltpu.VMEM((lanes, width), f32), pltpu.VMEM((lanes, share), f32)],
        compiler_params=params,
        name="field",
    )(moved.reshape(dir_total * lanes // 8, share), gathered, radiation, near)
    return field.transpose(0, 2, 1)


def solution(mesh):
    return jax.shard_map(
        local,
        mesh=mesh,
        in_specs=(
            P(None, "box", None),
            P(None, "box", None, "dir", None),
            P("box", None),
            P("box"),
            P(None, None, "box", "dir", None),
            P("dir", None),
            P("dir", None),
            P(None, None, "dir"),
            P(),
            P(),
            P(),
            P(None, None, "dir"),
        ),
        out_specs=P(None, "box", "dir"),
        check_vma=False,
    )
```

```python
import functools

import jax
import jax.numpy as jnp
from jax import lax
from jax.experimental import pallas as pl
from jax.experimental.pallas import tpu as pltpu
from jax.sharding import PartitionSpec as P

highest = lax.Precision.HIGHEST
f32 = jnp.float32
below, above = 1, 2
lead = 8
tall_window = 48
reach = below + above + 1
VMEM = pl.BlockSpec(memory_space=pltpu.VMEM)
SMEM = pl.BlockSpec(memory_space=pltpu.SMEM)
HBM = pl.BlockSpec(memory_space=pltpu.HBM)
params = pltpu.CompilerParams(vmem_limit_bytes=12 * 2**20)
alone = pltpu.CompilerParams(vmem_limit_bytes=60 * 2**20)


def sums_of_eight(tiles):
    row = lax.broadcasted_iota(jnp.int32, tiles[0].shape, 0)
    for step in (1, 2, 4):
        even = (row & step) == 0
        tiles = [
            jnp.where(even, a, b) + pltpu.roll(jnp.where(even, b, a), 8 - step, 0)
            for a, b in zip(tiles[0::2], tiles[1::2])
        ]
    return tiles[0]


def leaf_kernel(cuts, shares, total, spare, current, stencil, weight, shift, radiation, out, patterns, *scratch):
    given, points, weights, shifts, tables, columns, rows, samples, sems = scratch
    pols, boxes, own, width = radiation.shape[1:]
    step = boxes // cuts
    small = [
        pltpu.make_async_copy(source, target, sems.at[cuts + index])
        for index, (source, target) in enumerate(((current, given), (stencil, points), (weight, weights), (shift, shifts)))
    ]
    for copy in small:
        copy.start()
    copies = []
    for cut in range(cuts):
        part = pl.ds(cut * step, step)
        copy = pltpu.make_async_copy(radiation.at[:, :, part], patterns.at[:, :, part], sems.at[cut])
        copy.start()
        copies.append(copy)
    for copy in small:
        copy.wait()
    for part in range(2):
        columns[part] = given[part].T
    place = lax.axis_index("dir")
    mine = pl.ds(pl.multiple_of(place * own, own), own)
    piece = width // shares
    lanes = stencil.shape[1]
    tables[0:8, :] = shifts[0]
    tables[8:16, :] = shifts[1]
    tables[16:, :] = jnp.zeros((tables.shape[0] - 16, lanes), f32)
    centre = place * piece - below + lax.broadcasted_iota(jnp.int32, (1, lanes), 1) // (lanes // piece)
    for offset in range(reach):
        line = jnp.zeros((1, lanes), f32)
        for point in range(stencil.shape[0]):
            at = lax.rem(points[point : point + 1, :] - centre + width, width)
            line = line + jnp.where(at == offset, weights[point : point + 1, :], 0.0)
        tables[16 + offset : 17 + offset, :] = line
    begin = lax.rem(lax.axis_index("box") + total - lax.rem(place * (16 + reach), total), total)
    real, imag = columns[0, mine, :], columns[1, mine, :]
    for cut in range(cuts):
        copies[cut].wait()
        for group in range(cut * step, (cut + 1) * step, 8):
            eight = range(group, group + 8)
            cur_re = [jnp.broadcast_to(real[:, box : box + 1], (own, 128)) for box in eight]
            cur_im = [jnp.broadcast_to(imag[:, box : box + 1], (own, 128)) for box in eight]
            for pol in range(pols):
                for block in range(width // 128):
                    at = slice(block * 128, block * 128 + 128)
                    rad_re = [patterns[0, pol, box, :, at] for box in eight]
                    rad_im = [patterns[1, pol, box, :, at] for box in eight]
                    both = list(zip(rad_re, rad_im, cur_re, cur_im))
                    line = pol * boxes + group
                    rows[line : line + 8, at] = sums_of_eight([a * c - b * d for a, b, c, d in both])
                    line = (pols + pol) * boxes + group
                    rows[line : line + 8, at] = sums_of_eight([a * d + b * c for a, b, c, d in both])
    for block in range(width // 128):
        samples[lead + block * 128 : lead + block * 128 + 128, :] = rows[:, block * 128 : block * 128 + 128].T
    samples[lead - below : lead, :] = samples[lead + width - below : lead + width, :]
    samples[lead + width : lead + width + above, :] = samples[lead : lead + above, :]
    span = piece + below + above
    own_rows = [tables[pl.ds(begin + index * total, 1), :] for index in range(spare)]
    for share in range(shares):
        first, at = lead - below + share * piece, share * (span + spare)
        out[at : at + span, :] = samples[first : first + span, :]
        for index in range(spare):
            out[at + span + index : at + span + index + 1, :] = own_rows[index]


def plan_kernel(parents, width, piece, stencil, weight, source, kind, count, translation, interp, picks, factors, codes):
    lanes = stencil.shape[1]
    begin = lax.axis_index("dir") * piece - below
    row = lax.broadcasted_iota(jnp.int32, (128, lanes), 0)
    table = jnp.zeros((128, lanes), f32)
    for point in range(stencil.shape[0]):
        at = lax.rem(stencil[point : point + 1, :] - begin + width, width)
        table = table + jnp.where(row == at, weight[point : point + 1, :], 0.0)
    interp[...] = table
    kinds = translation.shape[1]
    slots, tops = source.shape
    lines, columns = picks.shape[0] // (kinds * parents), picks.shape[1]
    origin = source[...]
    spot = (origin // parents) * (lines * parents) + lax.rem(origin, parents)
    live = lax.broadcasted_iota(jnp.int32, (slots, tops), 0) < count[...]
    codes[...] = jnp.where(live, kind[...] * columns + spot, -1).astype(f32).T
    mine = codes[pl.ds(lax.axis_index("box") * parents, parents), :]
    own_kind = lax.broadcasted_iota(jnp.int32, (kinds * parents, slots), 0) // parents
    mine = jnp.concatenate([mine] * kinds, axis=0) - (own_kind * columns).astype(f32)
    lane = lax.broadcasted_iota(jnp.int32, (kinds * parents, columns), 1).astype(f32)
    counts = jnp.zeros((kinds * parents, columns), f32)
    for slot in range(slots):
        counts = counts + jnp.where(mine[:, slot : slot + 1] == lane, 1.0, 0.0)
    parts = [pltpu.roll(counts, line * parents, 1) if line else counts for line in range(lines)]
    picks[...] = jnp.concatenate(parts, axis=0).astype(jnp.bfloat16)
    for part in range(2):
        for which in range(kinds):
            one = translation[part, which : which + 1, :]
            factors[part, which * parents : (which + 1) * parents, :] = jnp.broadcast_to(one, (parents, lanes))


def lift_kernel(shares, copies, spare, received, interp, shift, out, total, tops):
    each = received.shape[0] // shares
    span = each - spare
    total[...] = jnp.zeros_like(total)
    part = received[0:span, :]
    for share in range(1, shares):
        part = part + received[share * each : share * each + span, :]
    total[0:span, :] = part
    up = jnp.dot(total[...].T, interp[...], precision=highest, preferred_element_type=f32)
    shift_re, shift_im = shift[0], shift[1]
    half = up.shape[0] // 2
    lines = half // 8
    for line in range(lines):
        up_re, up_im = up[line * 8 : line * 8 + 8], up[half + line * 8 : half + line * 8 + 8]
        tops[line : line + 1, :] = jnp.sum(up_re * shift_re - up_im * shift_im, axis=0, keepdims=True)
        tops[lines + line : lines + line + 1, :] = jnp.sum(up_re * shift_im + up_im * shift_re, axis=0, keepdims=True)
    height = tops.shape[0]
    place = lax.axis_index("box")
    for index in range(height - 2 * lines):
        number = place + index * copies
        share = number // (16 + reach)
        at = share * each + span + (number - share * (16 + reach)) // copies
        tops[2 * lines + index : 2 * lines + index + 1, :] = received[pl.ds(at, 1), :]
    value = tops[...]
    for copy in range(copies):
        out[copy * height : (copy + 1) * height, :] = value


def lower_kernel(shares, parents, picks, factors, gathered, out, compact):
    each = factors.shape[1]
    lines = picks.shape[0] // each
    pols = lines // 2
    height = lines * parents
    boxes = compact.shape[0] // height
    stride = gathered.shape[0] // boxes
    for box in range(boxes):
        compact[box * height : (box + 1) * height, :] = gathered[box * stride : box * stride + height, :]
    rest = compact[...]
    table = picks[...]
    raw = jnp.zeros((table.shape[0], rest.shape[1]), f32)
    for _ in range(3):
        part = rest.astype(jnp.bfloat16)
        raw = raw + jnp.dot(table, part, preferred_element_type=f32)
        rest = rest - part.astype(f32)

    def over_kinds(line, part):
        terms = raw[line * each : (line + 1) * each] * factors[part]
        total = terms[0:parents]
        for which in range(1, each // parents):
            total = total + terms[which * parents : (which + 1) * parents]
        return total

    moved = [over_kinds(pol, 0) - over_kinds(pols + pol, 1) for pol in range(pols)]
    moved += [over_kinds(pol, 1) + over_kinds(pols + pol, 0) for pol in range(pols)]
    value = jnp.concatenate(moved, axis=0)
    for share in range(shares):
        out[share * height : (share + 1) * height, :] = value


def near_kernel(neighbours, near_count, low, current, high, blocks, out, padded):
    slots, boxes = neighbours.shape
    first = lax.axis_index("box") * boxes - boxes
    for part in range(2):
        padded[part, 0:boxes, :] = low[part]
        padded[part, boxes : 2 * boxes, :] = current[part]
        padded[part, 2 * boxes : 3 * boxes, :] = high[part]
        padded[part, 3 * boxes :, :] = jnp.zeros((8, 128), f32)
    for box in range(boxes):
        used = near_count[box]
        sum_re = jnp.zeros(out.shape[2:], f32)
        sum_im = jnp.zeros(out.shape[2:], f32)
        for slot in range(slots):
            at = jnp.where(slot < used, neighbours[slot, box] - first, 3 * boxes)
            cur_re, cur_im = padded[0, pl.ds(at, 1), :], padded[1, pl.ds(at, 1), :]
            block_re, block_im = blocks[0, box, slot], blocks[1, box, slot]
            sum_re = sum_re + (block_re * cur_re - block_im * cur_im)
            sum_im = sum_im + (block_re * cur_im + block_im * cur_re)
        out[0, box] = sum_re
        out[1, box] = sum_im


def field_kernel(shares, total, received, gathered, radiation, near, out, samples, rows, down):
    pols, boxes, own, width = radiation.shape[1:]
    piece = width // shares
    height = received.shape[0] // shares
    half, tall = height // 2, down.shape[0] // 2
    stride = gathered.shape[0] // total
    lanes = received.shape[1]

    def table_row(number):
        return number % total * stride + height + number // total

    def octants(number):
        ends = [number]
        for one in range(number + 1, number + 8):
            if one % total == 0:
                ends.append(one)
        ends.append(number + 8)
        parts = []
        for low, high in zip(ends[:-1], ends[1:]):
            if high - low == 1:
                parts.append(gathered[table_row(low) : table_row(low) + 1, :])
            else:
                parts.append(gathered[pl.ds(table_row(low), high - low, stride=stride), :])
        return parts[0] if len(parts) == 1 else jnp.concatenate(parts, axis=0)

    samples[...] = jnp.zeros_like(samples)
    sample = lax.broadcasted_iota(jnp.int32, (tall_window, lanes), 0)
    offset = sample - lax.broadcasted_iota(jnp.int32, (tall_window, lanes), 1) // (lanes // piece)
    contract = (((1,), (1,)), ((), ()))
    for share in range(shares):
        number = share * (16 + reach)
        shift_re, shift_im = octants(number), octants(number + 8)
        table = jnp.zeros((tall_window, lanes), f32)
        for step in range(reach):
            at = table_row(number + 16 + step)
            table = jnp.where(offset == step, gathered[at : at + 1, :], table)
        for line in range(half):
            at = share * height + line
            moved_re, moved_im = received[at : at + 1, :], received[at + half : at + half + 1, :]
            down[line * 8 : line * 8 + 8, :] = moved_re * shift_re + moved_im * shift_im
            down[tall + line * 8 : tall + line * 8 + 8, :] = moved_im * shift_re - moved_re * shift_im
        value = down[...]
        value_hi = value.astype(jnp.bfloat16)
        value_lo = (value - value_hi.astype(f32)).astype(jnp.bfloat16)
        table_hi = table.astype(jnp.bfloat16)
        table_lo = (table - table_hi.astype(f32)).astype(jnp.bfloat16)
        tables = jnp.concatenate([table_hi, table_lo], axis=0)
        both = lax.dot_general(
            jnp.concatenate([tables, tables], axis=1),
            jnp.concatenate([value_hi, value_lo], axis=1),
            contract,
            preferred_element_type=f32,
        )
        settled = both[:tall_window] + both[tall_window:]
        first = lead - below + share * piece
        samples[first : first + tall_window, :] += settled
    samples[lead + width - below : lead + width, :] += samples[lead - below : lead, :]
    samples[lead : lead + above, :] += samples[lead + width : lead + width + above, :]
    for block in range(width // 128):
        rows[:, block * 128 : block * 128 + 128] = samples[lead + block * 128 : lead + block * 128 + 128, :].T
    lane = lax.broadcasted_iota(jnp.int32, (own, boxes), 1)
    all_re = jnp.zeros((own, boxes), f32)
    all_im = jnp.zeros((own, boxes), f32)
    for box in range(boxes):
        sum_re, sum_im = near[0, box], near[1, box]
        for pol in range(pols):
            at_re, at_im = pol * boxes + box, (pols + pol) * boxes + box
            for block in range(width // 128):
                cut = slice(block * 128, block * 128 + 128)
                in_re, in_im = rows[at_re : at_re + 1, cut], rows[at_im : at_im + 1, cut]
                rad_re, rad_im = radiation[0, pol, box, :, cut], radiation[1, pol, box, :, cut]
                sum_re = sum_re + (rad_re * in_re + rad_im * in_im)
                sum_im = sum_im + (rad_re * in_im - rad_im * in_re)
        all_re = jnp.where(lane == box, jnp.sum(sum_re, axis=1, keepdims=True), all_re)
        all_im = jnp.where(lane == box, jnp.sum(sum_im, axis=1, keepdims=True), all_im)
    out[0] = all_re
    out[1] = all_im


def local(
    current,
    near_block,
    neighbours,
    near_count,
    radiation,
    stencil,
    stencil_weight,
    child_shift,
    list_source,
    list_kind,
    list_count,
    translation,
):
    box_total, dir_total = lax.axis_size("box"), lax.axis_size("dir")
    _, pols, boxes, own, width = radiation.shape
    share = stencil.shape[0]
    parents = boxes // 8
    piece = width // dir_total
    span = piece + below + above
    lanes = 2 * pols * boxes
    held = lead + width + 16
    cuts = 4
    spare = -(-(16 + reach) // box_total)
    height = lanes // 8 + (16 + reach) * dir_total // box_total

    def shape(dims, dtype=f32):
        return jax.ShapeDtypeStruct(dims, dtype)

    forward = [(i, i + 1) for i in range(box_total - 1)]
    low = lax.ppermute(current, "box", forward)
    high = lax.ppermute(current, "box", [(b, a) for a, b in forward])

    windows = pl.pallas_call(
        functools.partial(leaf_kernel, cuts, dir_total, box_total, spare),
        out_shape=shape((dir_total * (span + spare), lanes)),
        in_specs=[HBM] * 5,
        out_specs=VMEM,
        scratch_shapes=[
            pltpu.VMEM(radiation.shape, f32),
            pltpu.VMEM(current.shape, f32),
            pltpu.VMEM((stencil.shape[1], share), jnp.int32),
            pltpu.VMEM((stencil.shape[1], share), f32),
            pltpu.VMEM(child_shift.shape, f32),
            pltpu.VMEM((spare * box_total + 16 + reach, share), f32),
            pltpu.VMEM((2, current.shape[2], boxes), f32),
            pltpu.VMEM((lanes, width), f32),
            pltpu.VMEM((held, lanes), f32),
            pltpu.SemaphoreType.DMA((cuts + 4,)),
        ],
        compiler_params=alone,
        name="leaf",
    )(current, stencil.T, stencil_weight.T, child_shift, radiation)
    windows = lax.all_to_all(windows.reshape(dir_total, 1, (span + spare) * lanes), "dir", 0, 0, tiled=True)

    kinds, tops_total = translation.shape[1], list_source.shape[0]
    interp, picks, factors = pl.pallas_call(
        functools.partial(plan_kernel, parents, width, piece),
        out_shape=(
            shape((128, share)),
            shape((2 * pols * kinds * parents, box_total * lanes // 8), dtype=jnp.bfloat16),
            shape((2, kinds * parents, share)),
        ),
        in_specs=[VMEM] * 6,
        out_specs=(VMEM, VMEM, VMEM),
        scratch_shapes=[pltpu.VMEM((tops_total, list_source.shape[1]), f32)],
        compiler_params=params,
        cost_estimate=pl.CostEstimate(flops=2_000_000, bytes_accessed=2_000_000, transcendentals=0),
        name="plan",
    )(stencil.T, stencil_weight.T, list_source.T, list_kind.T, list_count.reshape(1, -1), translation)

    near = pl.pallas_call(
        near_kernel,
        out_shape=shape((2, boxes, own, 128)),
        in_specs=[SMEM, SMEM] + [VMEM] * 4,
        out_specs=VMEM,
        scratch_shapes=[pltpu.VMEM((2, 3 * boxes + 8, 128), f32)],
        compiler_params=params,
        cost_estimate=pl.CostEstimate(flops=4_000_000, bytes_accessed=4_000_000, transcendentals=0),
        name="near",
    )(neighbours.T, near_count, low, current, high, near_block)

    tops = pl.pallas_call(
        functools.partial(lift_kernel, dir_total, box_total, spare),
        out_shape=shape((box_total * height, share)),
        in_specs=[VMEM] * 3,
        out_specs=VMEM,
        scratch_shapes=[pltpu.VMEM((128, lanes), f32), pltpu.VMEM((height, share), f32)],
        compiler_params=params,
        name="lift",
    )(windows.reshape(dir_total * (span + spare), lanes), interp, child_shift)
    gathered = lax.all_to_all(tops.reshape(box_total, 1, height * share), "box", 0, 0, tiled=True)
    gathered = gathered.reshape(box_total * height, share)

    moved = pl.pallas_call(
        functools.partial(lower_kernel, dir_total, parents),
        out_shape=shape((dir_total * lanes // 8, share)),
        in_specs=[VMEM] * 3,
        out_specs=VMEM,
        scratch_shapes=[pltpu.VMEM((box_total * lanes // 8, share), f32)],
        compiler_params=params,
        name="lower",
    )(picks, factors, gathered)
    moved = lax.all_to_all(moved.reshape(dir_total, 1, lanes // 8 * share), "dir", 0, 0, tiled=True)

    field = pl.pallas_call(
        functools.partial(field_kernel, dir_total, box_total),
        out_shape=shape((2, own, boxes)),
        in_specs=[VMEM] * 4,
        out_specs=VMEM,
        scratch_shapes=[pltpu.VMEM((held, lanes), f32), pltpu.VMEM((lanes, width), f32), pltpu.VMEM((lanes, share), f32)],
        compiler_params=params,
        name="field",
    )(moved.reshape(dir_total * lanes // 8, share), gathered, radiation, near)
    return field.transpose(0, 2, 1)


def solution(mesh):
    return jax.shard_map(
        local,
        mesh=mesh,
        in_specs=(
            P(None, "box", None),
            P(None, "box", None, "dir", None),
            P("box", None),
            P("box"),
            P(None, None, "box", "dir", None),
            P("dir", None),
            P("dir", None),
            P(None, None, "dir"),
            P(),
            P(),
            P(),
            P(None, None, "dir"),
        ),
        out_specs=P(None, "box", "dir"),
        check_vma=False,
    )
```

```python
import functools

import jax
import jax.numpy as jnp
from jax import lax
from jax.experimental import pallas as pl
from jax.experimental.pallas import tpu as pltpu
from jax.sharding import PartitionSpec as P

highest = lax.Precision.HIGHEST
f32 = jnp.float32
below, above = 1, 2
lead = 8
tall_window = 48
reach = below + above + 1
VMEM = pl.BlockSpec(memory_space=pltpu.VMEM)
SMEM = pl.BlockSpec(memory_space=pltpu.SMEM)
ANY = pl.BlockSpec(memory_space=pl.ANY)
HBM = pl.BlockSpec(memory_space=pltpu.HBM)
params = pltpu.CompilerParams(vmem_limit_bytes=12 * 2**20)
alone = pltpu.CompilerParams(vmem_limit_bytes=60 * 2**20)


def sums_of_eight(tiles):
    row = lax.broadcasted_iota(jnp.int32, tiles[0].shape, 0)
    for step in (1, 2, 4):
        even = (row & step) == 0
        tiles = [
            jnp.where(even, a, b) + pltpu.roll(jnp.where(even, b, a), 8 - step, 0)
            for a, b in zip(tiles[0::2], tiles[1::2])
        ]
    return tiles[0]


def leaf_kernel(cuts, shares, total, spare, current, stencil, weight, shift, radiation, out, patterns, *scratch):
    given, points, weights, shifts, tables, columns, rows, samples, sems = scratch
    pols, boxes, own, width = radiation.shape[1:]
    step = boxes // cuts
    small = [
        pltpu.make_async_copy(source, target, sems.at[cuts + index])
        for index, (source, target) in enumerate(((current, given), (stencil, points), (weight, weights), (shift, shifts)))
    ]
    copies = []
    for cut in range(cuts):
        part = pl.ds(cut * step, step)
        copy = pltpu.make_async_copy(radiation.at[:, :, part], patterns.at[:, :, part], sems.at[cut])
        copy.start()
        copies.append(copy)
        if cut == 0:
            for extra in small:
                extra.start()
    for copy in small:
        copy.wait()
    for part in range(2):
        columns[part] = given[part].T
    place = lax.axis_index("dir")
    mine = pl.ds(pl.multiple_of(place * own, own), own)
    piece = width // shares
    lanes = stencil.shape[1]
    tables[0:8, :] = shifts[0]
    tables[8:16, :] = shifts[1]
    tables[16:, :] = jnp.zeros((tables.shape[0] - 16, lanes), f32)
    centre = place * piece - below + lax.broadcasted_iota(jnp.int32, (1, lanes), 1) // (lanes // piece)
    for offset in range(reach):
        line = jnp.zeros((1, lanes), f32)
        for point in range(stencil.shape[0]):
            at = lax.rem(points[point : point + 1, :] - centre + width, width)
            line = line + jnp.where(at == offset, weights[point : point + 1, :], 0.0)
        tables[16 + offset : 17 + offset, :] = line
    begin = lax.rem(lax.axis_index("box") + total - lax.rem(place * (16 + reach), total), total)
    real, imag = columns[0, mine, :], columns[1, mine, :]
    for cut in range(cuts):
        copies[cut].wait()
        for group in range(cut * step, (cut + 1) * step, 8):
            eight = range(group, group + 8)
            cur_re = [jnp.broadcast_to(real[:, box : box + 1], (own, 128)) for box in eight]
            cur_im = [jnp.broadcast_to(imag[:, box : box + 1], (own, 128)) for box in eight]
            for pol in range(pols):
                for block in range(width // 128):
                    at = slice(block * 128, block * 128 + 128)
                    rad_re = [patterns[0, pol, box, :, at] for box in eight]
                    rad_im = [patterns[1, pol, box, :, at] for box in eight]
                    both = list(zip(rad_re, rad_im, cur_re, cur_im))
                    line = pol * boxes + group
                    rows[line : line + 8, at] = sums_of_eight([a * c - b * d for a, b, c, d in both])
                    line = (pols + pol) * boxes + group
                    rows[line : line + 8, at] = sums_of_eight([a * d + b * c for a, b, c, d in both])
    for block in range(width // 128):
        samples[lead + block * 128 : lead + block * 128 + 128, :] = rows[:, block * 128 : block * 128 + 128].T
    samples[lead - below : lead, :] = samples[lead + width - below : lead + width, :]
    samples[lead + width : lead + width + above, :] = samples[lead : lead + above, :]
    span = piece + below + above
    own_rows = [tables[pl.ds(begin + index * total, 1), :] for index in range(spare)]
    for share in range(shares):
        first, at = lead - below + share * piece, share * (span + spare)
        out[at : at + span, :] = samples[first : first + span, :]
        for index in range(spare):
            out[at + span + index : at + span + index + 1, :] = own_rows[index]


def plan_kernel(parents, width, piece, stencil, weight, source, kind, count, translation, interp, picks, factors, codes):
    lanes = stencil.shape[1]
    begin = lax.axis_index("dir") * piece - below
    row = lax.broadcasted_iota(jnp.int32, (128, lanes), 0)
    table = jnp.zeros((128, lanes), f32)
    for point in range(stencil.shape[0]):
        at = lax.rem(stencil[point : point + 1, :] - begin + width, width)
        table = table + jnp.where(row == at, weight[point : point + 1, :], 0.0)
    interp[...] = table
    kinds = translation.shape[1]
    slots, tops = source.shape
    lines, columns = picks.shape[0] // (kinds * parents), picks.shape[1]
    origin = source[...]
    spot = (origin // parents) * (lines * parents) + lax.rem(origin, parents)
    live = lax.broadcasted_iota(jnp.int32, (slots, tops), 0) < count[...]
    codes[...] = jnp.where(live, kind[...] * columns + spot, -1).astype(f32).T
    mine = codes[pl.ds(lax.axis_index("box") * parents, parents), :]
    own_kind = lax.broadcasted_iota(jnp.int32, (kinds * parents, slots), 0) // parents
    mine = jnp.concatenate([mine] * kinds, axis=0) - (own_kind * columns).astype(f32)
    lane = lax.broadcasted_iota(jnp.int32, (kinds * parents, columns), 1).astype(f32)
    counts = jnp.zeros((kinds * parents, columns), f32)
    for slot in range(slots):
        counts = counts + jnp.where(mine[:, slot : slot + 1] == lane, 1.0, 0.0)
    parts = [pltpu.roll(counts, line * parents, 1) if line else counts for line in range(lines)]
    picks[...] = jnp.concatenate(parts, axis=0).astype(jnp.bfloat16)
    for part in range(2):
        for which in range(kinds):
            one = translation[part, which : which + 1, :]
            factors[part, which * parents : (which + 1) * parents, :] = jnp.broadcast_to(one, (parents, lanes))


def lift_kernel(shares, copies, spare, received, interp, shift, near, out, total, tops):
    each = received.shape[0] // shares
    span = each - spare
    total[...] = jnp.zeros_like(total)
    part = received[0:span, :]
    for share in range(1, shares):
        part = part + received[share * each : share * each + span, :]
    total[0:span, :] = part
    up = jnp.dot(total[...].T, interp[...], precision=highest, preferred_element_type=f32)
    shift_re, shift_im = shift[0], shift[1]
    half = up.shape[0] // 2
    lines = half // 8
    for line in range(lines):
        up_re, up_im = up[line * 8 : line * 8 + 8], up[half + line * 8 : half + line * 8 + 8]
        tops[line : line + 1, :] = jnp.sum(up_re * shift_re - up_im * shift_im, axis=0, keepdims=True)
        tops[lines + line : lines + line + 1, :] = jnp.sum(up_re * shift_im + up_im * shift_re, axis=0, keepdims=True)
    height = tops.shape[0]
    place = lax.axis_index("box")
    for index in range(height - 2 * lines):
        number = place + index * copies
        share = number // (16 + reach)
        at = share * each + span + (number - share * (16 + reach)) // copies
        tops[2 * lines + index : 2 * lines + index + 1, :] = received[pl.ds(at, 1), :]
    value = tops[...]
    for copy in range(copies):
        out[copy * height : (copy + 1) * height, :] = value


def lower_kernel(shares, parents, picks, factors, gathered, out, compact):
    each = factors.shape[1]
    lines = picks.shape[0] // each
    pols = lines // 2
    height = lines * parents
    boxes = compact.shape[0] // height
    stride = gathered.shape[0] // boxes
    for box in range(boxes):
        compact[box * height : (box + 1) * height, :] = gathered[box * stride : box * stride + height, :]
    rest = compact[...]
    table = picks[...]
    raw = jnp.zeros((table.shape[0], rest.shape[1]), f32)
    for _ in range(3):
        part = rest.astype(jnp.bfloat16)
        raw = raw + jnp.dot(table, part, preferred_element_type=f32)
        rest = rest - part.astype(f32)

    def over_kinds(line, part):
        terms = raw[line * each : (line + 1) * each] * factors[part]
        total = terms[0:parents]
        for which in range(1, each // parents):
            total = total + terms[which * parents : (which + 1) * parents]
        return total

    moved = [over_kinds(pol, 0) - over_kinds(pols + pol, 1) for pol in range(pols)]
    moved += [over_kinds(pol, 1) + over_kinds(pols + pol, 0) for pol in range(pols)]
    value = jnp.concatenate(moved, axis=0)
    for share in range(shares):
        out[share * height : (share + 1) * height, :] = value


def near_kernel(neighbours, near_count, low, current, high, blocks, out, padded):
    slots, boxes = neighbours.shape
    first = lax.axis_index("box") * boxes - boxes
    for part in range(2):
        padded[part, 0:boxes, :] = low[part]
        padded[part, boxes : 2 * boxes, :] = current[part]
        padded[part, 2 * boxes : 3 * boxes, :] = high[part]
        padded[part, 3 * boxes :, :] = jnp.zeros((8, 128), f32)
    for box in range(boxes):
        used = near_count[box]
        sum_re = jnp.zeros(out.shape[2:], f32)
        sum_im = jnp.zeros(out.shape[2:], f32)
        for slot in range(slots):
            at = jnp.where(slot < used, neighbours[slot, box] - first, 3 * boxes)
            cur_re, cur_im = padded[0, pl.ds(at, 1), :], padded[1, pl.ds(at, 1), :]
            block_re, block_im = blocks[0, box, slot], blocks[1, box, slot]
            sum_re = sum_re + (block_re * cur_re - block_im * cur_im)
            sum_im = sum_im + (block_re * cur_im + block_im * cur_re)
        out[0, box] = sum_re
        out[1, box] = sum_im


def field_kernel(shares, total, received, gathered, radiation, near, out, samples, rows, down):
    pols, boxes, own, width = radiation.shape[1:]
    piece = width // shares
    height = received.shape[0] // shares
    half, tall = height // 2, down.shape[0] // 2
    stride = gathered.shape[0] // total
    lanes = received.shape[1]

    def table_row(number):
        return number % total * stride + height + number // total

    def octants(number):
        ends = [number]
        for one in range(number + 1, number + 8):
            if one % total == 0:
                ends.append(one)
        ends.append(number + 8)
        parts = []
        for low, high in zip(ends[:-1], ends[1:]):
            if high - low == 1:
                parts.append(gathered[table_row(low) : table_row(low) + 1, :])
            else:
                parts.append(gathered[pl.ds(table_row(low), high - low, stride=stride), :])
        return parts[0] if len(parts) == 1 else jnp.concatenate(parts, axis=0)

    samples[...] = jnp.zeros_like(samples)
    sample = lax.broadcasted_iota(jnp.int32, (tall_window, lanes), 0)
    offset = sample - lax.broadcasted_iota(jnp.int32, (tall_window, lanes), 1) // (lanes // piece)
    contract = (((1,), (1,)), ((), ()))
    for share in range(shares):
        number = share * (16 + reach)
        shift_re, shift_im = octants(number), octants(number + 8)
        table = jnp.zeros((tall_window, lanes), f32)
        for step in range(reach):
            at = table_row(number + 16 + step)
            table = jnp.where(offset == step, gathered[at : at + 1, :], table)
        for line in range(half):
            at = share * height + line
            moved_re, moved_im = received[at : at + 1, :], received[at + half : at + half + 1, :]
            down[line * 8 : line * 8 + 8, :] = moved_re * shift_re + moved_im * shift_im
            down[tall + line * 8 : tall + line * 8 + 8, :] = moved_im * shift_re - moved_re * shift_im
        value = down[...]
        value_hi = value.astype(jnp.bfloat16)
        value_lo = (value - value_hi.astype(f32)).astype(jnp.bfloat16)
        table_hi = table.astype(jnp.bfloat16)
        table_lo = (table - table_hi.astype(f32)).astype(jnp.bfloat16)
        tables = jnp.concatenate([table_hi, table_lo], axis=0)
        both = lax.dot_general(
            jnp.concatenate([tables, tables], axis=1),
            jnp.concatenate([value_hi, value_lo], axis=1),
            contract,
            preferred_element_type=f32,
        )
        settled = both[:tall_window] + both[tall_window:]
        first = lead - below + share * piece
        samples[first : first + tall_window, :] += settled
    samples[lead + width - below : lead + width, :] += samples[lead - below : lead, :]
    samples[lead : lead + above, :] += samples[lead + width : lead + width + above, :]
    for block in range(width // 128):
        rows[:, block * 128 : block * 128 + 128] = samples[lead + block * 128 : lead + block * 128 + 128, :].T
    lane = lax.broadcasted_iota(jnp.int32, (own, boxes), 1)
    all_re = jnp.zeros((own, boxes), f32)
    all_im = jnp.zeros((own, boxes), f32)
    for box in range(boxes):
        sum_re, sum_im = near[0, box], near[1, box]
        for pol in range(pols):
            at_re, at_im = pol * boxes + box, (pols + pol) * boxes + box
            for block in range(width // 128):
                cut = slice(block * 128, block * 128 + 128)
                in_re, in_im = rows[at_re : at_re + 1, cut], rows[at_im : at_im + 1, cut]
                rad_re, rad_im = radiation[0, pol, box, :, cut], radiation[1, pol, box, :, cut]
                sum_re = sum_re + (rad_re * in_re + rad_im * in_im)
                sum_im = sum_im + (rad_re * in_im - rad_im * in_re)
        all_re = jnp.where(lane == box, jnp.sum(sum_re, axis=1, keepdims=True), all_re)
        all_im = jnp.where(lane == box, jnp.sum(sum_im, axis=1, keepdims=True), all_im)
    out[0] = all_re
    out[1] = all_im


def local(
    current,
    near_block,
    neighbours,
    near_count,
    radiation,
    stencil,
    stencil_weight,
    child_shift,
    list_source,
    list_kind,
    list_count,
    translation,
):
    box_total, dir_total = lax.axis_size("box"), lax.axis_size("dir")
    _, pols, boxes, own, width = radiation.shape
    share = stencil.shape[0]
    parents = boxes // 8
    piece = width // dir_total
    span = piece + below + above
    lanes = 2 * pols * boxes
    held = lead + width + 16
    cuts = 4
    spare = -(-(16 + reach) // box_total)
    height = lanes // 8 + (16 + reach) * dir_total // box_total

    def shape(dims, dtype=f32):
        return jax.ShapeDtypeStruct(dims, dtype)

    forward = [(i, i + 1) for i in range(box_total - 1)]
    low = lax.ppermute(current, "box", forward)
    high = lax.ppermute(current, "box", [(b, a) for a, b in forward])

    windows = pl.pallas_call(
        functools.partial(leaf_kernel, cuts, dir_total, box_total, spare),
        out_shape=shape((dir_total * (span + spare), lanes)),
        in_specs=[HBM] * 5,
        out_specs=VMEM,
        scratch_shapes=[
            pltpu.VMEM(radiation.shape, f32),
            pltpu.VMEM(current.shape, f32),
            pltpu.VMEM((stencil.shape[1], share), jnp.int32),
            pltpu.VMEM((stencil.shape[1], share), f32),
            pltpu.VMEM(child_shift.shape, f32),
            pltpu.VMEM((spare * box_total + 16 + reach, share), f32),
            pltpu.VMEM((2, current.shape[2], boxes), f32),
            pltpu.VMEM((lanes, width), f32),
            pltpu.VMEM((held, lanes), f32),
            pltpu.SemaphoreType.DMA((cuts + 4,)),
        ],
        compiler_params=alone,
        name="leaf",
    )(current, stencil.T, stencil_weight.T, child_shift, radiation)
    windows = lax.all_to_all(windows.reshape(dir_total, 1, (span + spare) * lanes), "dir", 0, 0, tiled=True)

    kinds, tops_total = translation.shape[1], list_source.shape[0]
    interp, picks, factors = pl.pallas_call(
        functools.partial(plan_kernel, parents, width, piece),
        out_shape=(
            shape((128, share)),
            shape((2 * pols * kinds * parents, box_total * lanes // 8), dtype=jnp.bfloat16),
            shape((2, kinds * parents, share)),
        ),
        in_specs=[VMEM] * 6,
        out_specs=(VMEM, VMEM, VMEM),
        scratch_shapes=[pltpu.VMEM((tops_total, list_source.shape[1]), f32)],
        compiler_params=params,
        cost_estimate=pl.CostEstimate(flops=2_000_000, bytes_accessed=2_000_000, transcendentals=0),
        name="plan",
    )(stencil.T, stencil_weight.T, list_source.T, list_kind.T, list_count.reshape(1, -1), translation)

    near = pl.pallas_call(
        near_kernel,
        out_shape=shape((2, boxes, own, 128)),
        in_specs=[SMEM, SMEM] + [VMEM] * 4,
        out_specs=VMEM,
        scratch_shapes=[pltpu.VMEM((2, 3 * boxes + 8, 128), f32)],
        compiler_params=params,
        cost_estimate=pl.CostEstimate(flops=4_000_000, bytes_accessed=4_000_000, transcendentals=0),
        name="near",
    )(neighbours.T, near_count, low, current, high, near_block)

    tops = pl.pallas_call(
        functools.partial(lift_kernel, dir_total, box_total, spare),
        out_shape=shape((box_total * height, share)),
        in_specs=[VMEM] * 3 + [ANY],
        out_specs=VMEM,
        scratch_shapes=[pltpu.VMEM((128, lanes), f32), pltpu.VMEM((height, share), f32)],
        compiler_params=params,
        name="lift",
    )(windows.reshape(dir_total * (span + spare), lanes), interp, child_shift, near)
    gathered = lax.all_to_all(tops.reshape(box_total, 1, height * share), "box", 0, 0, tiled=True)
    gathered = gathered.reshape(box_total * height, share)

    moved = pl.pallas_call(
        functools.partial(lower_kernel, dir_total, parents),
        out_shape=shape((dir_total * lanes // 8, share)),
        in_specs=[VMEM] * 3,
        out_specs=VMEM,
        scratch_shapes=[pltpu.VMEM((box_total * lanes // 8, share), f32)],
        compiler_params=params,
        name="lower",
    )(picks, factors, gathered)
    moved = lax.all_to_all(moved.reshape(dir_total, 1, lanes // 8 * share), "dir", 0, 0, tiled=True)

    field = pl.pallas_call(
        functools.partial(field_kernel, dir_total, box_total),
        out_shape=shape((2, own, boxes)),
        in_specs=[VMEM] * 4,
        out_specs=VMEM,
        scratch_shapes=[pltpu.VMEM((held, lanes), f32), pltpu.VMEM((lanes, width), f32), pltpu.VMEM((lanes, share), f32)],
        compiler_params=params,
        name="field",
    )(moved.reshape(dir_total * lanes // 8, share), gathered, radiation, near)
    return field.transpose(0, 2, 1)


def solution(mesh):
    return jax.shard_map(
        local,
        mesh=mesh,
        in_specs=(
            P(None, "box", None),
            P(None, "box", None, "dir", None),
            P("box", None),
            P("box"),
            P(None, None, "box", "dir", None),
            P("dir", None),
            P("dir", None),
            P(None, None, "dir"),
            P(),
            P(),
            P(),
            P(None, None, "dir"),
        ),
        out_specs=P(None, "box", "dir"),
        check_vma=False,
    )
```

```python
import functools
import math

import jax
import jax.numpy as jnp
from jax import lax
from jax.experimental import pallas as pl
from jax.experimental.pallas import tpu as pltpu
from jax.sharding import PartitionSpec as P

highest = lax.Precision.HIGHEST
f32 = jnp.float32
below, above = 1, 2
lead = 8
tall_window = 48
reach = below + above + 1
VMEM = pl.BlockSpec(memory_space=pltpu.VMEM)
SMEM = pl.BlockSpec(memory_space=pltpu.SMEM)
ANY = pl.BlockSpec(memory_space=pl.ANY)
HBM = pl.BlockSpec(memory_space=pltpu.HBM)
params = pltpu.CompilerParams(vmem_limit_bytes=12 * 2**20)
alone = pltpu.CompilerParams(vmem_limit_bytes=60 * 2**20)


def sums_of_eight(tiles):
    row = lax.broadcasted_iota(jnp.int32, tiles[0].shape, 0)
    for step in (1, 2, 4):
        even = (row & step) == 0
        tiles = [
            jnp.where(even, a, b) + pltpu.roll(jnp.where(even, b, a), 8 - step, 0)
            for a, b in zip(tiles[0::2], tiles[1::2])
        ]
    return tiles[0]


def leaf_kernel(cuts, shares, total, spare, current, stencil, weight, shift, radiation, out, patterns, *scratch):
    given, points, weights, shifts, tables, columns, rows, samples, sems = scratch
    pols, boxes, own, width = radiation.shape[1:]
    step = boxes // cuts
    small = [
        pltpu.make_async_copy(source, target, sems.at[cuts + index])
        for index, (source, target) in enumerate(((current, given), (stencil, points), (weight, weights), (shift, shifts)))
    ]
    for copy in small:
        copy.start()
    copies = []
    for cut in range(cuts):
        part = pl.ds(cut * step, step)
        copy = pltpu.make_async_copy(radiation.at[:, :, part], patterns.at[:, :, part], sems.at[cut])
        copy.start()
        copies.append(copy)
    for copy in small:
        copy.wait()
    for part in range(2):
        columns[part] = given[part].T
    place = lax.axis_index("dir")
    mine = pl.ds(pl.multiple_of(place * own, own), own)
    piece = width // shares
    lanes = stencil.shape[1]
    tables[0:8, :] = shifts[0]
    tables[8:16, :] = shifts[1]
    tables[16:, :] = jnp.zeros((tables.shape[0] - 16, lanes), f32)
    centre = place * piece - below + lax.broadcasted_iota(jnp.int32, (1, lanes), 1) // (lanes // piece)
    for offset in range(reach):
        line = jnp.zeros((1, lanes), f32)
        for point in range(stencil.shape[0]):
            at = lax.rem(points[point : point + 1, :] - centre + width, width)
            line = line + jnp.where(at == offset, weights[point : point + 1, :], 0.0)
        tables[16 + offset : 17 + offset, :] = line
    begin = lax.rem(lax.axis_index("box") + total - lax.rem(place * (16 + reach), total), total)
    real, imag = columns[0, mine, :], columns[1, mine, :]
    for cut in range(cuts):
        copies[cut].wait()
        for group in range(cut * step, (cut + 1) * step, 8):
            eight = range(group, group + 8)
            cur_re = [jnp.broadcast_to(real[:, box : box + 1], (own, 128)) for box in eight]
            cur_im = [jnp.broadcast_to(imag[:, box : box + 1], (own, 128)) for box in eight]
            for pol in range(pols):
                for block in range(width // 128):
                    at = slice(block * 128, block * 128 + 128)
                    rad_re = [patterns[0, pol, box, :, at] for box in eight]
                    rad_im = [patterns[1, pol, box, :, at] for box in eight]
                    both = list(zip(rad_re, rad_im, cur_re, cur_im))
                    line = pol * boxes + group
                    rows[line : line + 8, at] = sums_of_eight([a * c - b * d for a, b, c, d in both])
                    line = (pols + pol) * boxes + group
                    rows[line : line + 8, at] = sums_of_eight([a * d + b * c for a, b, c, d in both])
    for block in range(width // 128):
        samples[lead + block * 128 : lead + block * 128 + 128, :] = rows[:, block * 128 : block * 128 + 128].T
    samples[lead - below : lead, :] = samples[lead + width - below : lead + width, :]
    samples[lead + width : lead + width + above, :] = samples[lead : lead + above, :]
    span = piece + below + above
    own_rows = [tables[pl.ds(begin + index * total, 1), :] for index in range(spare)]
    for share in range(shares):
        first, at = lead - below + share * piece, share * (span + spare)
        out[at : at + span, :] = samples[first : first + span, :]
        for index in range(spare):
            out[at + span + index : at + span + index + 1, :] = own_rows[index]


def plan_kernel(parents, width, piece, stencil, weight, source, kind, count, translation, interp, picks, factors, codes):
    lanes = stencil.shape[1]
    begin = lax.axis_index("dir") * piece - below
    row = lax.broadcasted_iota(jnp.int32, (128, lanes), 0)
    table = jnp.zeros((128, lanes), f32)
    for point in range(stencil.shape[0]):
        at = lax.rem(stencil[point : point + 1, :] - begin + width, width)
        table = table + jnp.where(row == at, weight[point : point + 1, :], 0.0)
    interp[...] = table
    kinds = translation.shape[1]
    slots, tops = source.shape
    lines, columns = picks.shape[0] // (kinds * parents), picks.shape[1]
    origin = source[...]
    spot = (origin // parents) * (lines * parents) + lax.rem(origin, parents)
    live = lax.broadcasted_iota(jnp.int32, (slots, tops), 0) < count[...]
    codes[...] = jnp.where(live, kind[...] * columns + spot, -1).astype(f32).T
    mine = codes[pl.ds(lax.axis_index("box") * parents, parents), :]
    own_kind = lax.broadcasted_iota(jnp.int32, (kinds * parents, slots), 0) // parents
    mine = jnp.concatenate([mine] * kinds, axis=0) - (own_kind * columns).astype(f32)
    lane = lax.broadcasted_iota(jnp.int32, (kinds * parents, columns), 1).astype(f32)
    counts = jnp.zeros((kinds * parents, columns), f32)
    for slot in range(slots):
        counts = counts + jnp.where(mine[:, slot : slot + 1] == lane, 1.0, 0.0)
    parts = [pltpu.roll(counts, line * parents, 1) if line else counts for line in range(lines)]
    picks[...] = jnp.concatenate(parts, axis=0).astype(jnp.bfloat16)
    for part in range(2):
        for which in range(kinds):
            one = translation[part, which : which + 1, :]
            factors[part, which * parents : (which + 1) * parents, :] = jnp.broadcast_to(one, (parents, lanes))


def lift_kernel(shares, copies, spare, received, interp, shift, near, out, total, tops, group):
    each = received.shape[0] // shares
    span = each - spare
    total[...] = jnp.zeros_like(total)
    part = received[0:span, :]
    for share in range(1, shares):
        part = part + received[share * each : share * each + span, :]
    total[0:span, :] = part
    up = jnp.dot(total[...].T, interp[...], precision=highest, preferred_element_type=f32)
    shift_re, shift_im = shift[0], shift[1]
    half = up.shape[0] // 2
    lines = half // 8
    for line in range(lines):
        up_re, up_im = up[line * 8 : line * 8 + 8], up[half + line * 8 : half + line * 8 + 8]
        tops[line : line + 1, :] = jnp.sum(up_re * shift_re - up_im * shift_im, axis=0, keepdims=True)
        tops[lines + line : lines + line + 1, :] = jnp.sum(up_re * shift_im + up_im * shift_re, axis=0, keepdims=True)
    height = tops.shape[0]
    place = lax.axis_index("box")
    for index in range(height - 2 * lines):
        number = place + index * copies
        share = number // (16 + reach)
        at = share * each + span + (number - share * (16 + reach)) // copies
        tops[2 * lines + index : 2 * lines + index + 1, :] = received[pl.ds(at, 1), :]
    value = tops[...]
    several = group.shape[0] // height
    for copy in range(several):
        group[copy * height : (copy + 1) * height, :] = value
    tiles = group[...]
    for copy in range(copies // several):
        out[copy * several * height : (copy + 1) * several * height, :] = tiles


def lower_kernel(shares, parents, picks, factors, gathered, out, compact):
    each = factors.shape[1]
    lines = picks.shape[0] // each
    pols = lines // 2
    height = lines * parents
    boxes = compact.shape[0] // height
    stride = gathered.shape[0] // boxes
    for box in range(boxes):
        compact[box * height : (box + 1) * height, :] = gathered[box * stride : box * stride + height, :]
    rest = compact[...]
    table = picks[...]
    raw = jnp.zeros((table.shape[0], rest.shape[1]), f32)
    for _ in range(3):
        part = rest.astype(jnp.bfloat16)
        raw = raw + jnp.dot(table, part, preferred_element_type=f32)
        rest = rest - part.astype(f32)

    def over_kinds(line, part):
        terms = raw[line * each : (line + 1) * each] * factors[part]
        total = terms[0:parents]
        for which in range(1, each // parents):
            total = total + terms[which * parents : (which + 1) * parents]
        return total

    moved = [over_kinds(pol, 0) - over_kinds(pols + pol, 1) for pol in range(pols)]
    moved += [over_kinds(pol, 1) + over_kinds(pols + pol, 0) for pol in range(pols)]
    value = jnp.concatenate(moved, axis=0)
    for share in range(shares):
        out[share * height : (share + 1) * height, :] = value


def near_kernel(neighbours, near_count, low, current, high, blocks, out, padded):
    slots, boxes = neighbours.shape
    first = lax.axis_index("box") * boxes - boxes
    for part in range(2):
        padded[part, 0:boxes, :] = low[part]
        padded[part, boxes : 2 * boxes, :] = current[part]
        padded[part, 2 * boxes : 3 * boxes, :] = high[part]
        padded[part, 3 * boxes :, :] = jnp.zeros((8, 128), f32)
    for box in range(boxes):
        used = near_count[box]
        sum_re = jnp.zeros(out.shape[2:], f32)
        sum_im = jnp.zeros(out.shape[2:], f32)
        for slot in range(slots):
            at = jnp.where(slot < used, neighbours[slot, box] - first, 3 * boxes)
            cur_re, cur_im = padded[0, pl.ds(at, 1), :], padded[1, pl.ds(at, 1), :]
            block_re, block_im = blocks[0, box, slot], blocks[1, box, slot]
            sum_re = sum_re + (block_re * cur_re - block_im * cur_im)
            sum_im = sum_im + (block_re * cur_im + block_im * cur_re)
        out[0, box] = sum_re
        out[1, box] = sum_im


def field_kernel(shares, total, received, gathered, radiation, near, out, samples, rows, down):
    pols, boxes, own, width = radiation.shape[1:]
    piece = width // shares
    height = received.shape[0] // shares
    half, tall = height // 2, down.shape[0] // 2
    stride = gathered.shape[0] // total
    lanes = received.shape[1]

    def table_row(number):
        return number % total * stride + height + number // total

    def octants(number):
        ends = [number]
        for one in range(number + 1, number + 8):
            if one % total == 0:
                ends.append(one)
        ends.append(number + 8)
        parts = []
        for low, high in zip(ends[:-1], ends[1:]):
            if high - low == 1:
                parts.append(gathered[table_row(low) : table_row(low) + 1, :])
            else:
                parts.append(gathered[pl.ds(table_row(low), high - low, stride=stride), :])
        return parts[0] if len(parts) == 1 else jnp.concatenate(parts, axis=0)

    samples[...] = jnp.zeros_like(samples)
    sample = lax.broadcasted_iota(jnp.int32, (tall_window, lanes), 0)
    offset = sample - lax.broadcasted_iota(jnp.int32, (tall_window, lanes), 1) // (lanes // piece)
    contract = (((1,), (1,)), ((), ()))
    for share in range(shares):
        number = share * (16 + reach)
        shift_re, shift_im = octants(number), octants(number + 8)
        table = jnp.zeros((tall_window, lanes), f32)
        for step in range(reach):
            at = table_row(number + 16 + step)
            table = jnp.where(offset == step, gathered[at : at + 1, :], table)
        for line in range(half):
            at = share * height + line
            moved_re, moved_im = received[at : at + 1, :], received[at + half : at + half + 1, :]
            down[line * 8 : line * 8 + 8, :] = moved_re * shift_re + moved_im * shift_im
            down[tall + line * 8 : tall + line * 8 + 8, :] = moved_im * shift_re - moved_re * shift_im
        value = down[...]
        value_hi = value.astype(jnp.bfloat16)
        value_lo = (value - value_hi.astype(f32)).astype(jnp.bfloat16)
        table_hi = table.astype(jnp.bfloat16)
        table_lo = (table - table_hi.astype(f32)).astype(jnp.bfloat16)
        tables = jnp.concatenate([table_hi, table_lo], axis=0)
        both = lax.dot_general(
            jnp.concatenate([tables, tables], axis=1),
            jnp.concatenate([value_hi, value_lo], axis=1),
            contract,
            preferred_element_type=f32,
        )
        settled = both[:tall_window] + both[tall_window:]
        first = lead - below + share * piece
        samples[first : first + tall_window, :] += settled
    samples[lead + width - below : lead + width, :] += samples[lead - below : lead, :]
    samples[lead : lead + above, :] += samples[lead + width : lead + width + above, :]
    for block in range(width // 128):
        rows[:, block * 128 : block * 128 + 128] = samples[lead + block * 128 : lead + block * 128 + 128, :].T
    lane = lax.broadcasted_iota(jnp.int32, (own, boxes), 1)
    all_re = jnp.zeros((own, boxes), f32)
    all_im = jnp.zeros((own, boxes), f32)
    for box in range(boxes):
        sum_re, sum_im = near[0, box], near[1, box]
        for pol in range(pols):
            at_re, at_im = pol * boxes + box, (pols + pol) * boxes + box
            for block in range(width // 128):
                cut = slice(block * 128, block * 128 + 128)
                in_re, in_im = rows[at_re : at_re + 1, cut], rows[at_im : at_im + 1, cut]
                rad_re, rad_im = radiation[0, pol, box, :, cut], radiation[1, pol, box, :, cut]
                sum_re = sum_re + (rad_re * in_re + rad_im * in_im)
                sum_im = sum_im + (rad_re * in_im - rad_im * in_re)
        all_re = jnp.where(lane == box, jnp.sum(sum_re, axis=1, keepdims=True), all_re)
        all_im = jnp.where(lane == box, jnp.sum(sum_im, axis=1, keepdims=True), all_im)
    out[0] = all_re
    out[1] = all_im


def local(
    current,
    near_block,
    neighbours,
    near_count,
    radiation,
    stencil,
    stencil_weight,
    child_shift,
    list_source,
    list_kind,
    list_count,
    translation,
):
    box_total, dir_total = lax.axis_size("box"), lax.axis_size("dir")
    _, pols, boxes, own, width = radiation.shape
    share = stencil.shape[0]
    parents = boxes // 8
    piece = width // dir_total
    span = piece + below + above
    lanes = 2 * pols * boxes
    held = lead + width + 16
    cuts = 4
    spare = -(-(16 + reach) // box_total)
    height = lanes // 8 + (16 + reach) * dir_total // box_total

    def shape(dims, dtype=f32):
        return jax.ShapeDtypeStruct(dims, dtype)

    forward = [(i, i + 1) for i in range(box_total - 1)]
    low = lax.ppermute(current, "box", forward)
    high = lax.ppermute(current, "box", [(b, a) for a, b in forward])

    windows = pl.pallas_call(
        functools.partial(leaf_kernel, cuts, dir_total, box_total, spare),
        out_shape=shape((dir_total * (span + spare), lanes)),
        in_specs=[HBM] * 5,
        out_specs=VMEM,
        scratch_shapes=[
            pltpu.VMEM(radiation.shape, f32),
            pltpu.VMEM(current.shape, f32),
            pltpu.VMEM((stencil.shape[1], share), jnp.int32),
            pltpu.VMEM((stencil.shape[1], share), f32),
            pltpu.VMEM(child_shift.shape, f32),
            pltpu.VMEM((spare * box_total + 16 + reach, share), f32),
            pltpu.VMEM((2, current.shape[2], boxes), f32),
            pltpu.VMEM((lanes, width), f32),
            pltpu.VMEM((held, lanes), f32),
            pltpu.SemaphoreType.DMA((cuts + 4,)),
        ],
        compiler_params=alone,
        name="leaf",
    )(current, stencil.T, stencil_weight.T, child_shift, radiation)
    windows = lax.all_to_all(windows.reshape(dir_total, 1, (span + spare) * lanes), "dir", 0, 0, tiled=True)

    kinds, tops_total = translation.shape[1], list_source.shape[0]
    interp, picks, factors = pl.pallas_call(
        functools.partial(plan_kernel, parents, width, piece),
        out_shape=(
            shape((128, share)),
            shape((2 * pols * kinds * parents, box_total * lanes // 8), dtype=jnp.bfloat16),
            shape((2, kinds * parents, share)),
        ),
        in_specs=[VMEM] * 6,
        out_specs=(VMEM, VMEM, VMEM),
        scratch_shapes=[pltpu.VMEM((tops_total, list_source.shape[1]), f32)],
        compiler_params=params,
        cost_estimate=pl.CostEstimate(flops=2_000_000, bytes_accessed=2_000_000, transcendentals=0),
        name="plan",
    )(stencil.T, stencil_weight.T, list_source.T, list_kind.T, list_count.reshape(1, -1), translation)

    near = pl.pallas_call(
        near_kernel,
        out_shape=shape((2, boxes, own, 128)),
        in_specs=[SMEM, SMEM] + [VMEM] * 4,
        out_specs=VMEM,
        scratch_shapes=[pltpu.VMEM((2, 3 * boxes + 8, 128), f32)],
        compiler_params=params,
        cost_estimate=pl.CostEstimate(flops=4_000_000, bytes_accessed=4_000_000, transcendentals=0),
        name="near",
    )(neighbours.T, near_count, low, current, high, near_block)

    tops = pl.pallas_call(
        functools.partial(lift_kernel, dir_total, box_total, spare),
        out_shape=shape((box_total * height, share)),
        in_specs=[VMEM] * 3 + [ANY],
        out_specs=VMEM,
        scratch_shapes=[
            pltpu.VMEM((128, lanes), f32),
            pltpu.VMEM((height, share), f32),
            pltpu.VMEM((height * math.gcd(box_total, 8 // math.gcd(height, 8)), share), f32),
        ],
        compiler_params=params,
        name="lift",
    )(windows.reshape(dir_total * (span + spare), lanes), interp, child_shift, near)
    gathered = lax.all_to_all(tops.reshape(box_total, 1, height * share), "box", 0, 0, tiled=True)
    gathered = gathered.reshape(box_total * height, share)

    moved = pl.pallas_call(
        functools.partial(lower_kernel, dir_total, parents),
        out_shape=shape((dir_total * lanes // 8, share)),
        in_specs=[VMEM] * 3,
        out_specs=VMEM,
        scratch_shapes=[pltpu.VMEM((box_total * lanes // 8, share), f32)],
        compiler_params=params,
        name="lower",
    )(picks, factors, gathered)
    moved = lax.all_to_all(moved.reshape(dir_total, 1, lanes // 8 * share), "dir", 0, 0, tiled=True)

    field = pl.pallas_call(
        functools.partial(field_kernel, dir_total, box_total),
        out_shape=shape((2, own, boxes)),
        in_specs=[VMEM] * 4,
        out_specs=VMEM,
        scratch_shapes=[pltpu.VMEM((held, lanes), f32), pltpu.VMEM((lanes, width), f32), pltpu.VMEM((lanes, share), f32)],
        compiler_params=params,
        name="field",
    )(moved.reshape(dir_total * lanes // 8, share), gathered, radiation, near)
    return field.transpose(0, 2, 1)


def solution(mesh):
    return jax.shard_map(
        local,
        mesh=mesh,
        in_specs=(
            P(None, "box", None),
            P(None, "box", None, "dir", None),
            P("box", None),
            P("box"),
            P(None, None, "box", "dir", None),
            P("dir", None),
            P("dir", None),
            P(None, None, "dir"),
            P(),
            P(),
            P(),
            P(None, None, "dir"),
        ),
        out_specs=P(None, "box", "dir"),
        check_vma=False,
    )
```
